256 devices in a mesh: clu: 64 (over z, y, core), row: 4 (over x).
Axes of the slice: x: 4, y: 4, z: 8, core: 2. Of those that a mesh axis runs over, the one named last changes fastest.
Arguments:
- embeddings: bfloat16 [131072, 1024], P(('clu', 'row')), may hold values from -400 to 400
- cluster: int32 [131072], P(('clu', 'row')), may hold values from 0 to 63, as said below
- doc_rank: int32 [131072], P(('clu', 'row')), may hold values from 0 to 131071, each once
Outputs:
- nearest_earlier: float32 [131072], P(('clu', 'row'))
The draws below stay inside these ranges and needn't reach their ends.
Inputs may be any that keep to these rules, and one draw needn't show every extreme that they name: The 512 documents of one device name any one cluster at most 16 times; one cluster is named exactly 16 times by every device, so it holds 4096 documents. `doc_rank`: all ranks differ.
All inputs are finite; a program needn't handle non-finite values.
Results may differ from the reference program's by a relative error of at most 0.00056.
Values may be sent and summed in bfloat16 or wider, within the bound.
No kernel may reach another device: no remote copies, remote signals or barrier semaphores. Data moves between devices by JAX's collectives and lax.ppermute only.
A program may use at most 64 MiB of HBM per device.

```python
import math
import jax
import jax.numpy as jnp
from jax import lax

D = 1024
ROWS_DEV = 512
CLUSTERS = 64
SEND = 16
DOCS = 131072
CAPC = 4096


def cluster_layout(key):
    key = jax.random.fold_in(key, 11)
    key_pref, key_fav, key_noise = jax.random.split(key, 3)
    blocks = DOCS // ROWS_DEV
    slot_count = CLUSTERS * SEND
    owner_of = jnp.arange(slot_count, dtype=jnp.int32) // SEND
    preference = jax.random.randint(key_pref, (CLUSTERS,), 0, 4).astype(jnp.int32) * 256
    favored = jax.random.randint(key_fav, (), 0, CLUSTERS)
    preference = preference.at[favored].set(262144)
    noise_pick = jax.random.randint(key_noise, (blocks, slot_count), 0, 1024).astype(jnp.int32)
    scores = (preference[owner_of][None, :] + noise_pick) * 4096 + jnp.arange(slot_count, dtype=jnp.int32)[None, :]
    _, picked = lax.top_k(scores, ROWS_DEV)
    return owner_of[picked].reshape(-1).astype(jnp.int32)


def draw_cluster(key, part):
    return cluster_layout(key)


def draw_embeddings(key, part):
    cluster = cluster_layout(key)
    key = jax.random.fold_in(key, 23)
    key_perm, key_shared, key_strength, key_noise, key_rows, key_cols = jax.random.split(key, 6)
    shuffle = jax.random.permutation(key_perm, DOCS).astype(jnp.int32)
    ordering = jnp.argsort(cluster * DOCS + shuffle, stable=True).astype(jnp.int32)
    sorted_cluster = cluster[ordering]
    positions = jnp.arange(DOCS, dtype=jnp.int32)
    partner = jnp.bitwise_xor(positions, 1)
    paired = sorted_cluster == sorted_cluster[partner]
    pair_of = jnp.zeros((DOCS,), jnp.int32).at[ordering].set(positions // 2)
    paired_doc = jnp.zeros((DOCS,), jnp.bool_).at[ordering].set(paired)
    strength = jax.random.uniform(key_strength, (DOCS // 2,), jnp.float32, 0.6, 2.0)
    noise_rows = jax.random.truncated_normal(key_noise, -4.0, 4.0, (DOCS, D), jnp.float32)
    shared = jax.random.truncated_normal(key_shared, -4.0, 4.0, (DOCS // 2, D), jnp.float32)
    row_scale = jnp.exp(jax.random.uniform(key_rows, (DOCS, 1), jnp.float32, 0.0, math.log(10.0)))
    columns = jnp.exp(jax.random.uniform(key_cols, (1, D), jnp.float32, 0.0, math.log(3.0)))
    weights_pair = jnp.where(paired_doc, strength[pair_of], 0.0)
    values = row_scale * columns * (noise_rows + weights_pair[:, None] * shared[pair_of])
    return values.astype(jnp.bfloat16)


def setup_inputs(seed: int = 0) -> dict:
    key_of = jax.random.split(jax.random.key(seed), 4)
    return {
        "embeddings": draw_embeddings(jax.random.fold_in(key_of[3], 71), 0),
        "cluster": draw_cluster(jax.random.fold_in(key_of[3], 71), 0),
        "doc_rank": jax.random.permutation(key_of[2], DOCS).astype(jnp.int32),
    }


def cluster_best(unit_sorted, rank_sorted, first_row, population):
    members = lax.dynamic_slice_in_dim(unit_sorted, first_row, CAPC, 0)
    member_ranks = lax.dynamic_slice_in_dim(rank_sorted, first_row, CAPC, 0)
    occupied = jnp.arange(CAPC, dtype=jnp.int32) < population
    scores = jnp.dot(members, members.T, preferred_element_type=jnp.float32)
    earlier = occupied[None, :] & (member_ranks[None, :] < member_ranks[:, None])
    return lax.optimization_barrier(jnp.max(jnp.where(earlier, scores, -1.0), axis=1))

def reference(embeddings, cluster, doc_rank):
    widened = embeddings.astype(jnp.float32)
    squares_eps = lax.optimization_barrier(jnp.sum(widened * widened, axis=1, keepdims=True)) + 1e-06
    unit_rows = (widened * lax.rsqrt(squares_eps)).astype(jnp.bfloat16)
    ordering = jnp.argsort(cluster, stable=True).astype(jnp.int32)
    counts = jnp.zeros((CLUSTERS,), jnp.int32).at[cluster].add(1)
    starts = (jnp.cumsum(counts) - counts).astype(jnp.int32)
    unit_sorted = jnp.concatenate([unit_rows[ordering], jnp.zeros((CAPC, D), unit_rows.dtype)], axis=0)
    rank_sorted = jnp.concatenate([doc_rank[ordering], jnp.zeros((CAPC,), jnp.int32)], axis=0)
    per_cluster = lax.map(lambda cluster_id: cluster_best(unit_sorted, rank_sorted, starts[cluster_id], counts[cluster_id]), jnp.arange(CLUSTERS, dtype=jnp.int32))
    sorted_cluster = cluster[ordering]
    within = jnp.arange(DOCS, dtype=jnp.int32) - starts[sorted_cluster]
    values = per_cluster[sorted_cluster, within]
    return jnp.zeros_like(values).at[ordering].set(values)
```

```python
import functools

import jax
import jax.numpy as jnp
from jax import lax
from jax.experimental import pallas as pl
from jax.experimental.pallas import tpu as pltpu
from jax.sharding import Mesh, PartitionSpec as P

NZ, NY, NC, NX = 8, 4, 2, 4
CHIPS = NZ * NY * NX
SLOTS = 16
HALF = 8
NO_RANK = 1 << 20
STEPS = ((0, 1), (0, -1), (1, 0), (-1, 0))
TORUS = ("z", "y", "x")
ALL = ("z", "y", "core", "x")
MIB = 2**20


def dot(a, b, dims):
    return lax.dot_general(a, b, (dims, ((), ())), preferred_element_type=jnp.float32)


def pack_kernel(group_ref, emb_ref, clu_ref, rank_ref, rows_ref, ranks_ref, home_ref, slot_ref):
    docs = emb_ref.shape[0]
    wide = emb_ref[...].astype(jnp.float32)
    squares = jnp.sum(wide * wide, axis=1, keepdims=True) + 1e-06
    unit = (wide * lax.rsqrt(squares)).astype(jnp.bfloat16)
    clu = clu_ref[...]
    z, y, xh = clu // 8, (clu // 2) % 4, clu % 2
    x = 2 * xh + (y + z) % 2
    home = (z * NY + y) * NX + x
    on_home = lax.broadcasted_iota(jnp.int32, (CHIPS, docs), 0) == home
    member = on_home.astype(jnp.bfloat16)
    ahead = lax.broadcasted_iota(jnp.int32, (docs, docs), 0) < lax.broadcasted_iota(
        jnp.int32, (docs, docs), 1
    )
    before = dot(member, ahead.astype(jnp.bfloat16), ((1,), (0,)))
    slot = jnp.sum(jnp.where(on_home, before, 0.0), axis=0, keepdims=True).astype(jnp.int32)
    home_ref[...] = home
    slot_ref[...] = slot
    rank = rank_ref[...]
    in_slot = lax.broadcasted_iota(jnp.int32, (SLOTS, docs), 0) == slot
    digits = (rank & 255, (rank >> 8) & 255, rank >> 16, jnp.ones_like(rank))
    cols = jnp.concatenate(
        [jnp.where(in_slot, d.astype(jnp.float32), 0.0) for d in digits], axis=0
    ).astype(jnp.bfloat16)
    placed = dot(member, cols, ((1,), (1,))).astype(jnp.int32)
    low, mid, high, there = (placed[:, i * SLOTS : (i + 1) * SLOTS] for i in range(4))
    ranks_ref[...] = jnp.where(there > 0, low + 256 * mid + 65536 * high, NO_RANK)
    group = group_ref[0]
    dy = jnp.where(group == 2, -1, jnp.where(group == 3, 1, 0))
    dx = jnp.where(group == 0, -1, jnp.where(group == 1, 1, 0))
    via = (z * NY + ((y + dy) & 3)) * NX + ((x + dx) & 3)
    at = jnp.where(slot < HALF, home * HALF + slot, via * HALF + slot - HALF)
    total = CHIPS * HALF
    pick = lax.broadcasted_iota(jnp.int32, (total, docs), 0) == at
    rows_ref[...] = dot(
        jnp.where(pick, 1.0, 0.0).astype(jnp.bfloat16), unit, ((1,), (0,))
    ).astype(jnp.bfloat16)


def pack(group, embeddings, cluster, doc_rank):
    docs, features = embeddings.shape
    vmem = pl.BlockSpec(memory_space=pltpu.VMEM)
    return pl.pallas_call(
        pack_kernel,
        out_shape=(
            jax.ShapeDtypeStruct((CHIPS * HALF, features), jnp.bfloat16),
            jax.ShapeDtypeStruct((CHIPS, SLOTS), jnp.int32),
            jax.ShapeDtypeStruct((1, docs), jnp.int32),
            jax.ShapeDtypeStruct((1, docs), jnp.int32),
        ),
        in_specs=[pl.BlockSpec(memory_space=pltpu.SMEM), vmem, vmem, vmem],
        out_specs=(vmem,) * 4,
        compiler_params=pltpu.CompilerParams(vmem_limit_bytes=40 * MIB),
        name="pack",
    )(group, embeddings, cluster, doc_rank)


def compare_kernel(plan, nq, nk, *refs):
    queries, q_ranks = refs[:nq], refs[nq : 2 * nq]
    keys, k_ranks = refs[2 * nq : 2 * nq + nk], refs[2 * nq + nk : 2 * nq + 2 * nk]
    outs = refs[2 * nq + 2 * nk : 3 * nq + 2 * nk]
    best, q_cols = refs[-2:]
    tile = 512
    for q, against in enumerate(plan):
        rows = queries[q].shape[0]
        best[...] = jnp.full(best.shape, -1.0, jnp.float32)
        q_cols[...] = jnp.transpose(jnp.broadcast_to(q_ranks[q][...], (128, rows)))
        for k in against:

            @pl.loop(0, rows // tile)
            def _(t, q=q, k=k):
                here = pl.ds(t * tile, tile)
                scores = dot(queries[q][here, :], keys[k][...], ((1,), (1,)))
                top = best[here, :]
                for c in range(keys[k].shape[0] // 128):
                    cols = slice(c * 128, (c + 1) * 128)
                    earlier = k_ranks[k][:, cols] < q_cols[here, :]
                    top = jnp.maximum(top, jnp.where(earlier, scores[:, cols], -1.0))
                best[here, :] = top

        outs[q][...] = jnp.max(jnp.transpose(best[...]), axis=0, keepdims=True)


def compare(queries, q_ranks, keys, k_ranks, plan, name):
    rows, features = queries[0].shape
    vmem = pl.BlockSpec(memory_space=pltpu.VMEM)
    args = [*queries, *q_ranks, *keys, *k_ranks]
    pairs = sum(rows * keys[k].shape[0] for against in plan for k in against)
    return pl.pallas_call(
        functools.partial(compare_kernel, plan, len(queries), len(keys)),
        out_shape=tuple(jax.ShapeDtypeStruct((1, rows), jnp.float32) for _ in queries),
        in_specs=[vmem] * len(args),
        out_specs=(vmem,) * len(queries),
        scratch_shapes=[pltpu.VMEM((rows, 128), jnp.float32), pltpu.VMEM((rows, 128), jnp.int32)],
        compiler_params=pltpu.CompilerParams(vmem_limit_bytes=48 * MIB),
        cost_estimate=pl.CostEstimate(
            flops=2 * pairs * features, bytes_accessed=8 * MIB, transcendentals=0
        ),
        name=name,
    )(*args)


def unpack_kernel(back_ref, home_ref, slot_ref, out_ref):
    docs = home_ref.shape[1]
    on_home = lax.broadcasted_iota(jnp.int32, (CHIPS, docs), 0) == home_ref[...]
    found = lax.dot_general(
        back_ref[...],
        on_home.astype(jnp.float32),
        (((0,), (0,)), ((), ())),
        precision=lax.Precision.HIGHEST,
        preferred_element_type=jnp.float32,
    )
    in_slot = lax.broadcasted_iota(jnp.int32, (SLOTS, docs), 0) == slot_ref[...]
    out_ref[...] = jnp.sum(jnp.where(in_slot, found, 0.0), axis=0, keepdims=True)


def unpack(back, home, slot):
    vmem = pl.BlockSpec(memory_space=pltpu.VMEM)
    return pl.pallas_call(
        unpack_kernel,
        out_shape=jax.ShapeDtypeStruct(home.shape, jnp.float32),
        in_specs=[vmem] * 3,
        out_specs=vmem,
        name="unpack",
    )(back, home, slot)


def to_home(step):
    dy, dx = step
    place = lambda z, y, c, x: ((z * NY + y) * NC + c) * NX + x
    return [
        (place(z, y, c, x), place(z, (y + dy) % NY, c, (x + dx) % NX))
        for z in range(NZ)
        for y in range(NY)
        for c in range(NC)
        for x in range(NX)
        if (x + y + z) % 2
    ]


def other_core(a):
    return lax.ppermute(a, "core", [(0, 1), (1, 0)])


def exchange(a):
    return lax.all_to_all(a, TORUS, split_axis=0, concat_axis=0, tiled=True)


def per_device(embeddings, cluster, doc_rank):
    docs, features = embeddings.shape
    group = (lax.axis_index("z") // 2).reshape(1)
    rows, ranks, home, slot = pack(
        group, embeddings, cluster.reshape(1, docs), doc_rank.reshape(1, docs)
    )
    rows = exchange(rows.reshape(CHIPS, HALF, features)).reshape(CHIPS * HALF, features)
    ranks = exchange(ranks)
    both = (ranks, other_core(ranks))
    rank_first = [r[:, :HALF].reshape(1, -1) for r in both]
    rank_last = [r[:, HALF:].reshape(1, -1) for r in both]
    part = rows.shape[0] // 4
    passed = [
        lax.ppermute(rows[i * part : (i + 1) * part], ALL, to_home(step))
        for i, step in enumerate(STEPS)
    ]
    first = [rows, other_core(rows)]
    [near] = compare([rows], [rank_first[0]], first, rank_first, ((0, 1),), "compare_first")
    last = jnp.concatenate(passed, axis=0)
    lasts = [last, other_core(last)]
    near_more, far = compare(
        [rows, last],
        [rank_first[0], rank_last[0]],
        [*lasts, *first],
        [*rank_last, *rank_first],
        ((0, 1), (0, 1, 2, 3)),
        "compare_last",
    )
    near = jnp.maximum(near, near_more)
    result = jnp.concatenate([near.reshape(CHIPS, HALF), far.reshape(CHIPS, HALF)], axis=1)
    return unpack(exchange(result), home, slot).reshape(docs)


def solution(mesh):
    torus = Mesh(mesh.devices.reshape(NZ, NY, NC, NX), ALL)
    placed = (P(ALL, None), P(ALL), P(ALL))
    return jax.shard_map(
        per_device, mesh=torus, in_specs=placed, out_specs=P(ALL), check_vma=False
    )
```

```python
import functools

import jax
import jax.numpy as jnp
from jax import lax
from jax.experimental import pallas as pl
from jax.experimental.pallas import tpu as pltpu
from jax.sharding import Mesh, PartitionSpec as P

NZ, NY, NC, NX = 8, 4, 2, 4
CHIPS = NZ * NY * NX
SLOTS = 16
HALF = 8
NO_RANK = 1 << 20
STEPS = ((0, 1), (0, -1), (1, 0), (-1, 0))
TORUS = ("z", "y", "x")
ALL = ("z", "y", "core", "x")
MIB = 2**20
TILE = 512


def dot(a, b, dims):
    return lax.dot_general(a, b, (dims, ((), ())), preferred_element_type=jnp.float32)


def digit_weights():
    which = lax.broadcasted_iota(jnp.int32, (128, 128), 0)
    weight = jnp.where(
        which == 0, 1, jnp.where(which == 1, 256, jnp.where(which == 2, 65536, -NO_RANK))
    )
    return jnp.where(which < 4, weight, 0).astype(jnp.float32).astype(jnp.bfloat16)


def pack_kernel(group_ref, emb_ref, clu_ref, rank_ref, rows_ref, home_ref, slot_ref):
    docs, features = emb_ref.shape
    wide = emb_ref[...].astype(jnp.float32)
    squares = jnp.sum(wide * wide, axis=1, keepdims=True) + 1e-06
    unit = (wide * lax.rsqrt(squares)).astype(jnp.bfloat16)
    clu = clu_ref[...]
    z, y, xh = clu // 8, (clu // 2) % 4, clu % 2
    x = 2 * xh + (y + z) % 2
    home = (z * NY + y) * NX + x
    on_home = lax.broadcasted_iota(jnp.int32, (CHIPS, docs), 0) == home
    member = on_home.astype(jnp.bfloat16)
    ahead = lax.broadcasted_iota(jnp.int32, (docs, docs), 0) < lax.broadcasted_iota(
        jnp.int32, (docs, docs), 1
    )
    before = dot(member, ahead.astype(jnp.bfloat16), ((1,), (0,)))
    slot = jnp.sum(jnp.where(on_home, before, 0.0), axis=0, keepdims=True).astype(jnp.int32)
    home_ref[...] = home
    slot_ref[...] = slot
    rank = rank_ref[...]
    which = lax.broadcasted_iota(jnp.int32, (128, docs), 0)
    digits = jnp.where(
        which == 0,
        rank & 255,
        jnp.where(which == 1, (rank >> 8) & 255, jnp.where(which == 2, rank >> 16, 1)),
    )
    digits = jnp.where(which < 4, digits, 0).astype(jnp.float32).astype(jnp.bfloat16)
    group = group_ref[0]
    dy = jnp.where(group == 2, -1, jnp.where(group == 3, 1, 0))
    dx = jnp.where(group == 0, -1, jnp.where(group == 1, 1, 0))
    via = (z * NY + ((y + dy) & 3)) * NX + ((x + dx) & 3)
    at = jnp.where(slot < HALF, home * HALF + slot, via * HALF + slot - HALF)
    pick = lax.broadcasted_iota(jnp.int32, (CHIPS * HALF, docs), 0) == at
    pick = jnp.where(pick, 1.0, 0.0).astype(jnp.bfloat16)
    rows_ref[:, :features] = dot(pick, unit, ((1,), (0,))).astype(jnp.bfloat16)
    rows_ref[:, features:] = dot(pick, digits, ((1,), (1,))).astype(jnp.bfloat16)


def pack(group, embeddings, cluster, doc_rank):
    docs, features = embeddings.shape
    vmem = pl.BlockSpec(memory_space=pltpu.VMEM)
    return pl.pallas_call(
        pack_kernel,
        out_shape=(
            jax.ShapeDtypeStruct((CHIPS * HALF, features + 128), jnp.bfloat16),
            jax.ShapeDtypeStruct((1, docs), jnp.int32),
            jax.ShapeDtypeStruct((1, docs), jnp.int32),
        ),
        in_specs=[pl.BlockSpec(memory_space=pltpu.SMEM), vmem, vmem, vmem],
        out_specs=(vmem,) * 3,
        compiler_params=pltpu.CompilerParams(vmem_limit_bytes=40 * MIB),
        name="pack",
    )(group, embeddings, cluster, doc_rank)


def compare_kernel(plan, sets, *refs):
    core_ref, refs = refs[0], list(refs[1:])
    pieces, start, outs, by_row, by_col, row_rank, col_rank, joined = ([] for _ in range(8))
    for n, _, _ in sets:
        pieces.append([refs.pop(0) for _ in range(n)])
    for _, has, _ in sets:
        start.append(refs.pop(0) if has else None)
    for _, _, wanted in sets:
        outs.append(refs.pop(0) if wanted else None)
    for _ in sets:
        by_row.append(refs.pop(0))
        by_col.append(refs.pop(0))
        row_rank.append(refs.pop(0))
        col_rank.append(refs.pop(0))
    weights = digit_weights()
    features = pieces[0][0].shape[1] - 128
    for i, (n, _, _) in enumerate(sets):
        if n > 1:
            whole = refs.pop(0)
            part = pieces[i][0].shape[0]
            for p, piece in enumerate(pieces[i]):
                whole[p * part : (p + 1) * part, :] = piece[...]
        else:
            whole = pieces[i][0]
        joined.append(whole)
        tail = whole[:, features:]
        row_rank[i][...] = dot(tail, weights, ((1,), (0,))) + float(NO_RANK)
        col_rank[i][...] = dot(weights[:, :8], tail, ((0,), (1,))) + float(NO_RANK)
        by_row[i][...] = jnp.full(by_row[i].shape, -1.0, jnp.float32)
        by_col[i][...] = jnp.full(by_col[i].shape, -1.0, jnp.float32)
    core = core_ref[0]
    for (q, qb), (k, kb), both in plan:
        q_at = pl.ds(pl.multiple_of((core if qb is None else qb) * TILE, TILE), TILE)
        k_at = pl.ds(pl.multiple_of((core if kb is None else kb) * TILE, TILE), TILE)
        scores = dot(joined[q][q_at, :features], joined[k][k_at, :features], ((1,), (1,)))
        q_rank = row_rank[q][q_at, :]
        top = by_row[q][q_at, :]
        k_rank = col_rank[k][0:1, k_at]
        side = []
        for c in range(TILE // 128):
            cols = slice(c * 128, (c + 1) * 128)
            part = scores[:, cols]
            earlier = k_rank[:, cols] < q_rank
            top = jnp.maximum(top, jnp.where(earlier, part, -1.0))
            if both:
                other = jnp.where(earlier, -1.0, part)
                side.append(jnp.max(other.reshape(TILE // 8, 8, 128), axis=0))
        by_row[q][q_at, :] = top
        if both:
            by_col[k][:, k_at] = jnp.maximum(by_col[k][:, k_at], jnp.concatenate(side, axis=1))
    for i, out in enumerate(outs):
        if out is not None:
            best = jnp.max(jnp.transpose(by_row[i][...]), axis=0, keepdims=True)
            best = jnp.maximum(best, jnp.max(by_col[i][...], axis=0, keepdims=True))
            if start[i] is not None:
                best = jnp.maximum(best, start[i][...])
            out[...] = best


def compare(core, sets, plan, name):
    wide = sets[0][0][0].shape[1]
    rows = [sum(a.shape[0] for a in arrays) for arrays, _, _ in sets]
    vmem = pl.BlockSpec(memory_space=pltpu.VMEM)
    args = [a for arrays, _, _ in sets for a in arrays]
    args += [best for _, best, _ in sets if best is not None]
    wanted = [n for n, (_, _, want) in zip(rows, sets) if want]
    scratch = []
    for n in rows:
        scratch += [
            pltpu.VMEM((n, 128), jnp.float32),
            pltpu.VMEM((8, n), jnp.float32),
            pltpu.VMEM((n, 128), jnp.float32),
            pltpu.VMEM((8, n), jnp.float32),
        ]
    scratch += [
        pltpu.VMEM((n, wide), jnp.bfloat16)
        for n, (arrays, _, _) in zip(rows, sets)
        if len(arrays) > 1
    ]
    return pl.pallas_call(
        functools.partial(
            compare_kernel,
            plan,
            [(len(arrays), best is not None, want) for arrays, best, want in sets],
        ),
        out_shape=tuple(jax.ShapeDtypeStruct((1, n), jnp.float32) for n in wanted),
        in_specs=[pl.BlockSpec(memory_space=pltpu.SMEM)] + [vmem] * len(args),
        out_specs=(vmem,) * len(wanted),
        scratch_shapes=scratch,
        compiler_params=pltpu.CompilerParams(vmem_limit_bytes=48 * MIB),
        cost_estimate=pl.CostEstimate(
            flops=2 * len(plan) * TILE * TILE * wide,
            bytes_accessed=2 * wide * sum(rows),
            transcendentals=0,
        ),
        name=name,
    )(core, *args)


def unpack_kernel(back_ref, home_ref, slot_ref, out_ref):
    docs = home_ref.shape[1]
    on_home = lax.broadcasted_iota(jnp.int32, (CHIPS, docs), 0) == home_ref[...]
    found = lax.dot_general(
        back_ref[...],
        on_home.astype(jnp.float32),
        (((0,), (0,)), ((), ())),
        precision=lax.Precision.HIGHEST,
        preferred_element_type=jnp.float32,
    )
    in_slot = lax.broadcasted_iota(jnp.int32, (SLOTS, docs), 0) == slot_ref[...]
    out_ref[...] = jnp.sum(jnp.where(in_slot, found, 0.0), axis=0, keepdims=True)


def unpack(back, home, slot):
    vmem = pl.BlockSpec(memory_space=pltpu.VMEM)
    return pl.pallas_call(
        unpack_kernel,
        out_shape=jax.ShapeDtypeStruct(home.shape, jnp.float32),
        in_specs=[vmem] * 3,
        out_specs=vmem,
        name="unpack",
    )(back, home, slot)


def to_home(step):
    dy, dx = step
    place = lambda z, y, c, x: ((z * NY + y) * NC + c) * NX + x
    return [
        (place(z, y, c, x), place(z, (y + dy) % NY, c, (x + dx) % NX))
        for z in range(NZ)
        for y in range(NY)
        for c in range(NC)
        for x in range(NX)
        if (x + y + z) % 2
    ]


def other_core(a):
    return lax.ppermute(a, "core", [(0, 1), (1, 0)])


def exchange(a):
    return lax.all_to_all(a, TORUS, split_axis=0, concat_axis=0, tiled=True)


def per_device(embeddings, cluster, doc_rank):
    docs, features = embeddings.shape
    group = (lax.axis_index("z") // 2).reshape(1)
    core = lax.axis_index("core").reshape(1)
    rows, home, slot = pack(group, embeddings, cluster.reshape(1, docs), doc_rank.reshape(1, docs))
    wide = features + 128
    near = exchange(rows.reshape(CHIPS, HALF, wide)).reshape(CHIPS * HALF, wide)
    part = near.shape[0] // 4
    far = [
        lax.ppermute(near[i * part : (i + 1) * part], ALL, to_home(step))
        for i, step in enumerate(STEPS)
    ]
    near_there = other_core(near)
    plan = (
        ((0, 0), (0, 0), False),
        ((0, 1), (0, 1), False),
        ((0, 0), (0, 1), True),
        ((0, 0), (1, 1), True),
        ((0, None), (1, None), True),
    )
    best_near, best_near_there = compare(
        core, [([near], None, True), ([near_there], None, True)], plan, "compare_near"
    )
    far_there = [other_core(a) for a in far]
    plan = (
        ((0, 0), (0, 0), False),
        ((0, 1), (0, 1), False),
        ((0, 0), (0, 1), True),
        *(((0, q), (k, b), True) for q in (0, 1) for k in (1, 2) for b in (0, 1)),
    )
    best_far, best_near, best_near_there = compare(
        core,
        [(far, None, True), ([near], best_near, True), ([near_there], best_near_there, True)],
        plan,
        "compare_far",
    )
    plan = (((0, 0), (1, 1), True), ((0, None), (1, None), True))
    best_far, best_far_there = compare(
        core, [(far, best_far, True), (far_there, None, True)], plan, "compare_cores"
    )
    mine = jnp.concatenate([best_near, best_far], axis=0)
    theirs = other_core(jnp.concatenate([best_near_there, best_far_there], axis=0))
    result = jnp.maximum(mine, theirs).reshape(2, CHIPS, HALF)
    result = jnp.concatenate([result[0], result[1]], axis=1)
    return unpack(exchange(result), home, slot).reshape(docs)


def solution(mesh):
    torus = Mesh(mesh.devices.reshape(NZ, NY, NC, NX), ALL)
    placed = (P(ALL, None), P(ALL), P(ALL))
    return jax.shard_map(
        per_device, mesh=torus, in_specs=placed, out_specs=P(ALL), check_vma=False
    )
```

```python
import functools

import jax
import jax.numpy as jnp
from jax import lax
from jax.experimental import pallas as pl
from jax.experimental.pallas import tpu as pltpu
from jax.sharding import Mesh, PartitionSpec as P

NZ, NY, NC, NX = 8, 4, 2, 4
CHIPS, COLUMNS, HOMES = NZ * NY * NX, NY * NX, NZ // 2
SLOTS = 16
NO_RANK = 1 << 20
NEAR, FAR = (0, 1, 7, 2), (6, 3, 5, 4)
TORUS = ("z", "y", "x")
PLANE = ("y", "x")
ALL = ("z", "y", "core", "x")
MIB = 2**20
TILE = 512
PIECE = COLUMNS * SLOTS


def dot(a, b, dims):
    return lax.dot_general(a, b, (dims, ((), ())), preferred_element_type=jnp.float32)


def digit_weights():
    which = lax.broadcasted_iota(jnp.int32, (128, 128), 0)
    weight = jnp.where(
        which == 0, 1, jnp.where(which == 1, 256, jnp.where(which == 2, 65536, -NO_RANK))
    )
    return jnp.where(which < 4, weight, 0).astype(jnp.float32).astype(jnp.bfloat16)


def pack_kernel(place_ref, emb_ref, clu_ref, rank_ref, rows_ref, home_ref, slot_ref):
    docs, features = emb_ref.shape
    wide = emb_ref[...].astype(jnp.float32)
    squares = jnp.sum(wide * wide, axis=1, keepdims=True) + 1e-06
    unit = (wide * lax.rsqrt(squares)).astype(jnp.bfloat16)
    clu = clu_ref[...]
    column, which_home = clu // HOMES, clu % HOMES
    home = which_home * 2 * COLUMNS + column
    on_home = lax.broadcasted_iota(jnp.int32, (CHIPS, docs), 0) == home
    member = on_home.astype(jnp.bfloat16)
    ahead = lax.broadcasted_iota(jnp.int32, (docs, docs), 0) < lax.broadcasted_iota(
        jnp.int32, (docs, docs), 1
    )
    before = dot(member, ahead.astype(jnp.bfloat16), ((1,), (0,)))
    slot = jnp.sum(jnp.where(on_home, before, 0.0), axis=0, keepdims=True).astype(jnp.int32)
    home_ref[...] = home
    slot_ref[...] = slot
    rank = rank_ref[...]
    which = lax.broadcasted_iota(jnp.int32, (128, docs), 0)
    digits = jnp.where(
        which == 0,
        rank & 255,
        jnp.where(which == 1, (rank >> 8) & 255, jnp.where(which == 2, rank >> 16, 1)),
    )
    digits = jnp.where(which < 4, digits, 0).astype(jnp.float32).astype(jnp.bfloat16)
    ahead_of_z = (which_home - (place_ref[1] + 1) // 2) & (HOMES - 1)
    at = (column * HOMES + ahead_of_z) * SLOTS + slot
    pick = lax.broadcasted_iota(jnp.int32, (rows_ref.shape[0], docs), 0) == at
    pick = jnp.where(pick, 1.0, 0.0).astype(jnp.bfloat16)
    rows_ref[:, :features] = dot(pick, unit, ((1,), (0,))).astype(jnp.bfloat16)
    rows_ref[:, features:] = dot(pick, digits, ((1,), (1,))).astype(jnp.bfloat16)


def pack(place, embeddings, cluster, doc_rank):
    docs, features = embeddings.shape
    vmem = pl.BlockSpec(memory_space=pltpu.VMEM)
    return pl.pallas_call(
        pack_kernel,
        out_shape=(
            jax.ShapeDtypeStruct((COLUMNS * HOMES * SLOTS, features + 128), jnp.bfloat16),
            jax.ShapeDtypeStruct((1, docs), jnp.int32),
            jax.ShapeDtypeStruct((1, docs), jnp.int32),
        ),
        in_specs=[pl.BlockSpec(memory_space=pltpu.SMEM), vmem, vmem, vmem],
        out_specs=(vmem,) * 3,
        compiler_params=pltpu.CompilerParams(vmem_limit_bytes=40 * MIB),
        name="pack",
    )(place, embeddings, cluster, doc_rank)


def compare_kernel(plan, sets, order, *refs):
    place_ref, refs = refs[0], list(refs[1:])
    pieces, start, outs = [], [], []
    for n, _ in sets:
        pieces.append([refs.pop(0) for _ in range(n)])
    for _, has in sets:
        start.append(refs.pop(0) if has else None)
    if order is None:
        outs = [refs.pop(0) for _ in sets]
    else:
        outs = [refs.pop(0) for _ in range(2)]
    scratch = [None if n == 0 else [refs.pop(0) for _ in range(5)] for n, _ in sets]
    weights = digit_weights()
    for held, buffers in zip(pieces, scratch):
        if not held:
            continue
        whole, by_row, by_col, row_rank, col_rank = buffers
        features = whole.shape[1] - 128
        part = held[0].shape[0]
        for p, piece in enumerate(held):
            whole[p * part : (p + 1) * part, :] = piece[...]
        tail = whole[:, features:]
        row_rank[...] = dot(tail, weights, ((1,), (0,))) + float(NO_RANK)
        col_rank[...] = dot(weights[:, :8], tail, ((0,), (1,))) + float(NO_RANK)
        by_row[...] = jnp.full(by_row.shape, -1.0, jnp.float32)
        by_col[...] = jnp.full(by_col.shape, -1.0, jnp.float32)
    core = place_ref[0]
    for (q, qb), (k, kb), both in plan:
        q_rows, by_row, _, row_rank, _ = scratch[q]
        k_rows, _, by_col, _, col_rank = scratch[k]
        q_at = pl.ds(pl.multiple_of((core if qb is None else qb) * TILE, TILE), TILE)
        k_at = pl.ds(pl.multiple_of((core if kb is None else kb) * TILE, TILE), TILE)
        scores = dot(q_rows[q_at, :features], k_rows[k_at, :features], ((1,), (1,)))
        q_rank = row_rank[q_at, :]
        top = by_row[q_at, :]
        k_rank = col_rank[0:1, k_at]
        side = []
        for c in range(TILE // 128):
            cols = slice(c * 128, (c + 1) * 128)
            part = scores[:, cols]
            earlier = k_rank[:, cols] < q_rank
            top = jnp.maximum(top, jnp.where(earlier, part, -1.0))
            if both:
                other = jnp.where(earlier, -1.0, part)
                side.append(jnp.max(other.reshape(TILE // 8, 8, 128), axis=0))
        by_row[q_at, :] = top
        if both:
            by_col[:, k_at] = jnp.maximum(by_col[:, k_at], jnp.concatenate(side, axis=1))
    for i, buffers in enumerate(scratch):
        best = None if start[i] is None else start[i][...]
        if buffers is not None:
            _, by_row, by_col, _, _ = buffers
            found = jnp.max(jnp.transpose(by_row[...]), axis=0, keepdims=True)
            found = jnp.maximum(found, jnp.max(by_col[...], axis=0, keepdims=True))
            best = found if best is None else jnp.maximum(best, found)
        if order is None:
            outs[i][...] = best
        else:
            which, steps = order[i]
            for p, step in enumerate(steps):
                came = (place_ref[1] - step) & (NZ - 1)
                outs[which][pl.ds(came, 1), :] = best[:, p * PIECE : (p + 1) * PIECE]


def compare(place, sets, plan, order, name):
    wide = sets[0][0][0].shape[1]
    rows = [sum(a.shape[0] for a in arrays) for arrays, _ in sets]
    vmem = pl.BlockSpec(memory_space=pltpu.VMEM)
    args = [a for arrays, _ in sets for a in arrays]
    args += [best for _, best in sets if best is not None]
    shapes = [(1, n) for n in rows] if order is None else [(NZ, PIECE)] * 2
    scratch = []
    for n in rows:
        if n:
            scratch += [
                pltpu.VMEM((n, wide), jnp.bfloat16),
                pltpu.VMEM((n, 128), jnp.float32),
                pltpu.VMEM((8, n), jnp.float32),
                pltpu.VMEM((n, 128), jnp.float32),
                pltpu.VMEM((8, n), jnp.float32),
            ]
    return pl.pallas_call(
        functools.partial(
            compare_kernel, plan, [(len(arrays), best is not None) for arrays, best in sets], order
        ),
        out_shape=tuple(jax.ShapeDtypeStruct(shape, jnp.float32) for shape in shapes),
        in_specs=[pl.BlockSpec(memory_space=pltpu.SMEM)] + [vmem] * len(args),
        out_specs=(vmem,) * len(shapes),
        scratch_shapes=scratch,
        compiler_params=pltpu.CompilerParams(vmem_limit_bytes=48 * MIB),
        cost_estimate=pl.CostEstimate(
            flops=2 * len(plan) * TILE * TILE * wide,
            bytes_accessed=2 * wide * sum(rows),
            transcendentals=0,
        ),
        name=name,
    )(place, *args)


def unpack_kernel(back_ref, home_ref, slot_ref, out_ref):
    docs = home_ref.shape[1]
    on_home = lax.broadcasted_iota(jnp.int32, (CHIPS, docs), 0) == home_ref[...]
    found = lax.dot_general(
        back_ref[...],
        on_home.astype(jnp.float32),
        (((0,), (0,)), ((), ())),
        precision=lax.Precision.HIGHEST,
        preferred_element_type=jnp.float32,
    )
    in_slot = lax.broadcasted_iota(jnp.int32, (SLOTS, docs), 0) == slot_ref[...]
    out_ref[...] = jnp.sum(jnp.where(in_slot, found, 0.0), axis=0, keepdims=True)


def unpack(back, home, slot):
    vmem = pl.BlockSpec(memory_space=pltpu.VMEM)
    return pl.pallas_call(
        unpack_kernel,
        out_shape=jax.ShapeDtypeStruct(home.shape, jnp.float32),
        in_specs=[vmem] * 3,
        out_specs=vmem,
        name="unpack",
    )(back, home, slot)


def up_z(a, step):
    pairs = [(z, (z + step) % NZ) for z in range(NZ) if (z + step) % 2 == 0]
    return lax.ppermute(a, "z", pairs)


def other_core(a):
    return lax.ppermute(a, "core", [(0, 1), (1, 0)])


def exchange(a, axes):
    return lax.all_to_all(a, axes, split_axis=0, concat_axis=0, tiled=True)


def per_device(embeddings, cluster, doc_rank):
    docs, features = embeddings.shape
    wide = features + 128
    place = jnp.stack([lax.axis_index("core"), lax.axis_index("z")]).astype(jnp.int32)
    rows, home, slot = pack(place, embeddings, cluster.reshape(1, docs), doc_rank.reshape(1, docs))
    rows = exchange(rows.reshape(COLUMNS, HOMES * SLOTS, wide), PLANE)
    rows = rows.reshape(COLUMNS, HOMES, SLOTS, wide)
    parts = [rows[:, h].reshape(PIECE, wide) for h in range(HOMES)]
    arrive = lambda steps: [up_z(parts[s // 2], s) if s else parts[0] for s in steps]
    near, far = arrive(NEAR), arrive(FAR)
    near_there = [other_core(a) for a in near]
    plan = (
        ((0, 0), (0, 0), False),
        ((0, 1), (0, 1), False),
        ((0, 0), (0, 1), True),
        ((0, 0), (1, 1), True),
        ((0, None), (1, None), True),
    )
    best_near, best_near_there = compare(
        place, [(near, None), (near_there, None)], plan, None, "compare_near"
    )
    far_there = [other_core(a) for a in far]
    plan = (
        ((0, 0), (0, 0), False),
        ((0, 1), (0, 1), False),
        ((0, 0), (0, 1), True),
        *(((0, q), (k, b), True) for q in (0, 1) for k in (1, 2) for b in (0, 1)),
    )
    best_far, best_near, best_near_there = compare(
        place,
        [(far, None), (near, best_near), (near_there, best_near_there)],
        plan,
        None,
        "compare_far",
    )
    plan = (((0, 0), (1, 1), True), ((0, None), (1, None), True))
    mine, theirs = compare(
        place,
        [(far, best_far), (far_there, None), ([], best_near), ([], best_near_there)],
        plan,
        ((0, FAR), (1, FAR), (0, NEAR), (1, NEAR)),
        "compare_cores",
    )
    result = jnp.maximum(mine, other_core(theirs)).reshape(CHIPS, SLOTS)
    return unpack(exchange(result, TORUS), home, slot).reshape(docs)


def solution(mesh):
    torus = Mesh(mesh.devices.reshape(NZ, NY, NC, NX), ALL)
    placed = (P(ALL, None), P(ALL), P(ALL))
    return jax.shard_map(
        per_device, mesh=torus, in_specs=placed, out_specs=P(ALL), check_vma=False
    )
```

```python
import functools

import jax
import jax.numpy as jnp
from jax import lax
from jax.experimental import pallas as pl
from jax.experimental.pallas import tpu as pltpu
from jax.sharding import Mesh, PartitionSpec as P

NZ, NY, NC, NX = 8, 4, 2, 4
CHIPS = NZ * NY * NX
SLOTS = 16
HALF = 8
NO_RANK = 1 << 20
STEPS = ((0, 1), (0, -1), (1, 0), (-1, 0))
TORUS = ("z", "y", "x")
ALL = ("z", "y", "core", "x")
MIB = 2**20
TILE = 512


def dot(a, b, dims):
    return lax.dot_general(a, b, (dims, ((), ())), preferred_element_type=jnp.float32)


def digit_weights():
    which = lax.broadcasted_iota(jnp.int32, (128, 128), 0)
    weight = jnp.where(
        which == 0, 1, jnp.where(which == 1, 256, jnp.where(which == 2, 65536, -NO_RANK))
    )
    return jnp.where(which < 4, weight, 0).astype(jnp.float32).astype(jnp.bfloat16)


def pack_kernel(group_ref, emb_ref, labels_ref, rows_ref, home_ref, slot_ref):
    docs, features = emb_ref.shape
    wide = emb_ref[...].astype(jnp.float32)
    squares = jnp.sum(wide * wide, axis=1, keepdims=True) + 1e-06
    unit = (wide * lax.rsqrt(squares)).astype(jnp.bfloat16)
    clu = labels_ref[0:1, :]
    z, y, xh = clu // 8, (clu // 2) % 4, clu % 2
    x = 2 * xh + (y + z) % 2
    home = (z * NY + y) * NX + x
    on_home = lax.broadcasted_iota(jnp.int32, (CHIPS, docs), 0) == home
    member = on_home.astype(jnp.bfloat16)
    ahead = lax.broadcasted_iota(jnp.int32, (docs, docs), 0) < lax.broadcasted_iota(
        jnp.int32, (docs, docs), 1
    )
    before = dot(member, ahead.astype(jnp.bfloat16), ((1,), (0,)))
    slot = jnp.sum(jnp.where(on_home, before, 0.0), axis=0, keepdims=True).astype(jnp.int32)
    home_ref[...] = home
    slot_ref[...] = slot
    rank = labels_ref[1:2, :]
    which = lax.broadcasted_iota(jnp.int32, (128, docs), 0)
    digits = jnp.where(
        which == 0,
        rank & 255,
        jnp.where(which == 1, (rank >> 8) & 255, jnp.where(which == 2, rank >> 16, 1)),
    )
    digits = jnp.where(which < 4, digits, 0).astype(jnp.float32).astype(jnp.bfloat16)
    group = group_ref[0]
    dy = jnp.where(group == 2, -1, jnp.where(group == 3, 1, 0))
    dx = jnp.where(group == 0, -1, jnp.where(group == 1, 1, 0))
    via = (z * NY + ((y + dy) & 3)) * NX + ((x + dx) & 3)
    at = jnp.where(slot < HALF, home * HALF + slot, via * HALF + slot - HALF)
    pick = lax.broadcasted_iota(jnp.int32, (CHIPS * HALF, docs), 0) == at
    pick = jnp.where(pick, 1.0, 0.0).astype(jnp.bfloat16)
    rows_ref[:, :features] = dot(pick, unit, ((1,), (0,))).astype(jnp.bfloat16)
    rows_ref[:, features:] = dot(pick, digits, ((1,), (1,))).astype(jnp.bfloat16)


def pack(group, embeddings, labels):
    docs, features = embeddings.shape
    vmem = pl.BlockSpec(memory_space=pltpu.VMEM)
    return pl.pallas_call(
        pack_kernel,
        out_shape=(
            jax.ShapeDtypeStruct((CHIPS * HALF, features + 128), jnp.bfloat16),
            jax.ShapeDtypeStruct((1, docs), jnp.int32),
            jax.ShapeDtypeStruct((1, docs), jnp.int32),
        ),
        in_specs=[pl.BlockSpec(memory_space=pltpu.SMEM), vmem, vmem],
        out_specs=(vmem,) * 3,
        compiler_params=pltpu.CompilerParams(vmem_limit_bytes=24 * MIB),
        name="pack",
    )(group, embeddings, labels)


def compare_kernel(plan, sets, *refs):
    core_ref, refs = refs[0], list(refs[1:])
    pieces, start, outs, by_row, by_col, row_rank, col_rank, joined = ([] for _ in range(8))
    for n, _, _ in sets:
        pieces.append([refs.pop(0) for _ in range(n)])
    for _, has, _ in sets:
        start.append(refs.pop(0) if has else None)
    for _, _, wanted in sets:
        outs.append(refs.pop(0) if wanted else None)
    for _ in sets:
        by_row.append(refs.pop(0))
        by_col.append(refs.pop(0))
        row_rank.append(refs.pop(0))
        col_rank.append(refs.pop(0))
    weights = digit_weights()
    features = pieces[0][0].shape[1] - 128
    for i, (n, _, _) in enumerate(sets):
        if n > 1:
            whole = refs.pop(0)
            part = pieces[i][0].shape[0]
            for p, piece in enumerate(pieces[i]):
                whole[p * part : (p + 1) * part, :] = piece[...]
        else:
            whole = pieces[i][0]
        joined.append(whole)
        tail = whole[:, features:]
        row_rank[i][...] = dot(tail, weights, ((1,), (0,))) + float(NO_RANK)
        col_rank[i][...] = dot(weights[:, :8], tail, ((0,), (1,))) + float(NO_RANK)
        by_row[i][...] = jnp.full(by_row[i].shape, -1.0, jnp.float32)
        by_col[i][...] = jnp.full(by_col[i].shape, -1.0, jnp.float32)
    core = core_ref[0]
    for (q, qb), (k, kb), both in plan:
        q_at = pl.ds(pl.multiple_of((core if qb is None else qb) * TILE, TILE), TILE)
        k_at = pl.ds(pl.multiple_of((core if kb is None else kb) * TILE, TILE), TILE)
        scores = dot(joined[q][q_at, :features], joined[k][k_at, :features], ((1,), (1,)))
        q_rank = row_rank[q][q_at, :]
        top = by_row[q][q_at, :]
        k_rank = col_rank[k][0:1, k_at]
        side = []
        for c in range(TILE // 128):
            cols = slice(c * 128, (c + 1) * 128)
            part = scores[:, cols]
            earlier = k_rank[:, cols] < q_rank
            top = jnp.maximum(top, jnp.where(earlier, part, -1.0))
            if both:
                other = jnp.where(earlier, -1.0, part)
                side.append(jnp.max(other.reshape(TILE // 8, 8, 128), axis=0))
        by_row[q][q_at, :] = top
        if both:
            by_col[k][:, k_at] = jnp.maximum(by_col[k][:, k_at], jnp.concatenate(side, axis=1))
    for i, out in enumerate(outs):
        if out is not None:
            best = jnp.max(jnp.transpose(by_row[i][...]), axis=0, keepdims=True)
            best = jnp.maximum(best, jnp.max(by_col[i][...], axis=0, keepdims=True))
            if start[i] is not None:
                best = jnp.maximum(best, start[i][...])
            out[...] = best


def compare(core, sets, plan, name):
    wide = sets[0][0][0].shape[1]
    rows = [sum(a.shape[0] for a in arrays) for arrays, _, _ in sets]
    vmem = pl.BlockSpec(memory_space=pltpu.VMEM)
    args = [a for arrays, _, _ in sets for a in arrays]
    args += [best for _, best, _ in sets if best is not None]
    wanted = [n for n, (_, _, want) in zip(rows, sets) if want]
    scratch = []
    for n in rows:
        scratch += [
            pltpu.VMEM((n, 128), jnp.float32),
            pltpu.VMEM((8, n), jnp.float32),
            pltpu.VMEM((n, 128), jnp.float32),
            pltpu.VMEM((8, n), jnp.float32),
        ]
    scratch += [
        pltpu.VMEM((n, wide), jnp.bfloat16)
        for n, (arrays, _, _) in zip(rows, sets)
        if len(arrays) > 1
    ]
    return pl.pallas_call(
        functools.partial(
            compare_kernel,
            plan,
            [(len(arrays), best is not None, want) for arrays, best, want in sets],
        ),
        out_shape=tuple(jax.ShapeDtypeStruct((1, n), jnp.float32) for n in wanted),
        in_specs=[pl.BlockSpec(memory_space=pltpu.SMEM)] + [vmem] * len(args),
        out_specs=(vmem,) * len(wanted),
        scratch_shapes=scratch,
        compiler_params=pltpu.CompilerParams(vmem_limit_bytes=24 * MIB),
        cost_estimate=pl.CostEstimate(
            flops=2 * len(plan) * TILE * TILE * wide,
            bytes_accessed=2 * wide * sum(rows),
            transcendentals=0,
        ),
        name=name,
    )(core, *args)


def unpack_kernel(back_ref, home_ref, slot_ref, out_ref):
    docs = home_ref.shape[1]
    on_home = lax.broadcasted_iota(jnp.int32, (CHIPS, docs), 0) == home_ref[...]
    found = lax.dot_general(
        back_ref[...],
        on_home.astype(jnp.float32),
        (((0,), (0,)), ((), ())),
        precision=lax.Precision.HIGHEST,
        preferred_element_type=jnp.float32,
    )
    in_slot = lax.broadcasted_iota(jnp.int32, (SLOTS, docs), 0) == slot_ref[...]
    out_ref[...] = jnp.sum(jnp.where(in_slot, found, 0.0), axis=0, keepdims=True)


def unpack(back, home, slot):
    vmem = pl.BlockSpec(memory_space=pltpu.VMEM)
    return pl.pallas_call(
        unpack_kernel,
        out_shape=jax.ShapeDtypeStruct(home.shape, jnp.float32),
        in_specs=[vmem] * 3,
        out_specs=vmem,
        name="unpack",
    )(back, home, slot)


def to_home(step):
    dy, dx = step
    place = lambda z, y, c, x: ((z * NY + y) * NC + c) * NX + x
    return [
        (place(z, y, c, x), place(z, (y + dy) % NY, c, (x + dx) % NX))
        for z in range(NZ)
        for y in range(NY)
        for c in range(NC)
        for x in range(NX)
        if (x + y + z) % 2
    ]


def other_core(a):
    return lax.ppermute(a, "core", [(0, 1), (1, 0)])


def exchange(a):
    return lax.all_to_all(a, TORUS, split_axis=0, concat_axis=0, tiled=True)


def per_device(embeddings, cluster, doc_rank):
    docs, features = embeddings.shape
    group = (lax.axis_index("z") // 2).reshape(1)
    core = lax.axis_index("core").reshape(1)
    rows, home, slot = pack(group, embeddings, jnp.stack([cluster, doc_rank]))
    wide = features + 128
    near = exchange(rows.reshape(CHIPS, HALF, wide)).reshape(CHIPS * HALF, wide)
    part = near.shape[0] // 4
    far = [
        lax.ppermute(near[i * part : (i + 1) * part], ALL, to_home(step))
        for i, step in enumerate(STEPS)
    ]
    near_there = other_core(near)
    plan = (
        ((0, 0), (0, 0), False),
        ((0, 1), (0, 1), False),
        ((0, 0), (0, 1), True),
        ((0, 0), (1, 1), True),
        ((0, None), (1, None), True),
    )
    best_near, best_near_there = compare(
        core, [([near], None, True), ([near_there], None, True)], plan, "compare_near"
    )
    far, best_near, best_near_there = lax.optimization_barrier((far, best_near, best_near_there))
    far_there = [other_core(a) for a in far]
    plan = (
        ((0, 0), (0, 0), False),
        ((0, 1), (0, 1), False),
        ((0, 0), (0, 1), True),
        *(((0, q), (k, b), True) for q in (0, 1) for k in (1, 2) for b in (0, 1)),
    )
    best_far, best_near, best_near_there = compare(
        core,
        [(far, None, True), ([near], best_near, True), ([near_there], best_near_there, True)],
        plan,
        "compare_far",
    )
    plan = (((0, 0), (1, 1), True), ((0, None), (1, None), True))
    best_far, best_far_there = compare(
        core, [(far, best_far, True), (far_there, None, True)], plan, "compare_cores"
    )
    mine = jnp.concatenate([best_near, best_far], axis=0)
    theirs = other_core(jnp.concatenate([best_near_there, best_far_there], axis=0))
    result = jnp.maximum(mine, theirs).reshape(2, CHIPS, HALF)
    result = jnp.concatenate([result[0], result[1]], axis=1)
    return unpack(exchange(result), home, slot).reshape(docs)


def solution(mesh):
    torus = Mesh(mesh.devices.reshape(NZ, NY, NC, NX), ALL)
    placed = (P(ALL, None), P(ALL), P(ALL))
    return jax.shard_map(
        per_device, mesh=torus, in_specs=placed, out_specs=P(ALL), check_vma=False
    )
```

```python
import functools

import jax
import jax.numpy as jnp
from jax import lax
from jax.experimental import pallas as pl
from jax.experimental.pallas import tpu as pltpu
from jax.sharding import Mesh, PartitionSpec as P

NZ, NY, NC, NX = 8, 4, 2, 4
CHIPS = NZ * NY * NX
SLOTS = 16
HALF = 8
NO_RANK = 1 << 20
TORUS = ("z", "y", "x")
ALL = ("z", "y", "core", "x")
MIB = 2**20
TILE = 512


def dot(a, b, dims):
    return lax.dot_general(a, b, (dims, ((), ())), preferred_element_type=jnp.float32)


def digit_weights():
    which = lax.broadcasted_iota(jnp.int32, (128, 128), 0)
    weight = jnp.where(
        which == 0, 1, jnp.where(which == 1, 256, jnp.where(which == 2, 65536, -NO_RANK))
    )
    return jnp.where(which < 4, weight, 0).astype(jnp.float32).astype(jnp.bfloat16)


def pack_kernel(place_ref, emb_ref, labels_ref, rows_ref, home_ref, slot_ref):
    docs, features = emb_ref.shape
    wide = emb_ref[...].astype(jnp.float32)
    squares = jnp.sum(wide * wide, axis=1, keepdims=True) + 1e-06
    unit = (wide * lax.rsqrt(squares)).astype(jnp.bfloat16)
    clu = labels_ref[0:1, :]
    z, y, xh = clu // 8, (clu // 2) % 4, clu % 2
    x = 2 * xh + (y + z) % 2
    home = (z * NY + y) * NX + x
    on_home = lax.broadcasted_iota(jnp.int32, (CHIPS, docs), 0) == home
    member = on_home.astype(jnp.bfloat16)
    ahead = lax.broadcasted_iota(jnp.int32, (docs, docs), 0) < lax.broadcasted_iota(
        jnp.int32, (docs, docs), 1
    )
    before = dot(member, ahead.astype(jnp.bfloat16), ((1,), (0,)))
    slot = jnp.sum(jnp.where(on_home, before, 0.0), axis=0, keepdims=True).astype(jnp.int32)
    home_ref[...] = home
    slot_ref[...] = slot
    rank = labels_ref[1:2, :]
    which = lax.broadcasted_iota(jnp.int32, (128, docs), 0)
    digits = jnp.where(
        which == 0,
        rank & 255,
        jnp.where(which == 1, (rank >> 8) & 255, jnp.where(which == 2, rank >> 16, 1)),
    )
    digits = jnp.where(which < 4, digits, 0).astype(jnp.float32).astype(jnp.bfloat16)
    core, upper = place_ref[0], place_ref[1]
    side = jnp.where(upper == 0, -1, 1)
    dy, dx = side * core, side * (1 - core)
    via = (z * NY + ((y + dy) & 3)) * NX + ((x + dx) & 3)
    at = jnp.where(slot < HALF, home * HALF + slot, via * HALF + slot - HALF)
    pick = lax.broadcasted_iota(jnp.int32, (CHIPS * HALF, docs), 0) == at
    pick = jnp.where(pick, 1.0, 0.0).astype(jnp.bfloat16)
    rows_ref[:, :features] = dot(pick, unit, ((1,), (0,))).astype(jnp.bfloat16)
    rows_ref[:, features:] = dot(pick, digits, ((1,), (1,))).astype(jnp.bfloat16)


def pack(place, embeddings, labels):
    docs, features = embeddings.shape
    vmem = pl.BlockSpec(memory_space=pltpu.VMEM)
    return pl.pallas_call(
        pack_kernel,
        out_shape=(
            jax.ShapeDtypeStruct((CHIPS * HALF, features + 128), jnp.bfloat16),
            jax.ShapeDtypeStruct((1, docs), jnp.int32),
            jax.ShapeDtypeStruct((1, docs), jnp.int32),
        ),
        in_specs=[pl.BlockSpec(memory_space=pltpu.SMEM), vmem, vmem],
        out_specs=(vmem,) * 3,
        compiler_params=pltpu.CompilerParams(vmem_limit_bytes=24 * MIB),
        name="pack",
    )(place, embeddings, labels)


def compare_kernel(plan, sets, *refs):
    core_ref, refs = refs[0], list(refs[1:])
    pieces, start, outs, by_row, by_col, row_rank, col_rank, joined = ([] for _ in range(8))
    for n, _, _ in sets:
        pieces.append([refs.pop(0) for _ in range(n)])
    for _, has, _ in sets:
        start.append(refs.pop(0) if has else None)
    for _, _, wanted in sets:
        outs.append(refs.pop(0) if wanted else None)
    for _ in sets:
        by_row.append(refs.pop(0))
        by_col.append(refs.pop(0))
        row_rank.append(refs.pop(0))
        col_rank.append(refs.pop(0))
    weights = digit_weights()
    features = pieces[0][0].shape[1] - 128
    for i, (n, _, _) in enumerate(sets):
        if n > 1:
            whole = refs.pop(0)
            part = pieces[i][0].shape[0]
            for p, piece in enumerate(pieces[i]):
                whole[p * part : (p + 1) * part, :] = piece[...]
        else:
            whole = pieces[i][0]
        joined.append(whole)
        tail = whole[:, features:]
        row_rank[i][...] = dot(tail, weights, ((1,), (0,))) + float(NO_RANK)
        col_rank[i][...] = dot(weights[:, :8], tail, ((0,), (1,))) + float(NO_RANK)
        by_row[i][...] = jnp.full(by_row[i].shape, -1.0, jnp.float32)
        by_col[i][...] = jnp.full(by_col[i].shape, -1.0, jnp.float32)
    core = core_ref[0]
    for (q, qb), (k, kb), both in plan:
        q_at = pl.ds(pl.multiple_of((core if qb is None else qb) * TILE, TILE), TILE)
        k_at = pl.ds(pl.multiple_of((core if kb is None else kb) * TILE, TILE), TILE)
        scores = dot(joined[q][q_at, :features], joined[k][k_at, :features], ((1,), (1,)))
        q_rank = row_rank[q][q_at, :]
        top = by_row[q][q_at, :]
        k_rank = col_rank[k][0:1, k_at]
        side = []
        for c in range(TILE // 128):
            cols = slice(c * 128, (c + 1) * 128)
            part = scores[:, cols]
            earlier = k_rank[:, cols] < q_rank
            top = jnp.maximum(top, jnp.where(earlier, part, -1.0))
            if both:
                other = jnp.where(earlier, -1.0, part)
                side.append(jnp.max(other.reshape(TILE // 8, 8, 128), axis=0))
        by_row[q][q_at, :] = top
        if both:
            by_col[k][:, k_at] = jnp.maximum(by_col[k][:, k_at], jnp.concatenate(side, axis=1))
    for i, out in enumerate(outs):
        if out is not None:
            best = jnp.max(jnp.transpose(by_row[i][...]), axis=0, keepdims=True)
            best = jnp.maximum(best, jnp.max(by_col[i][...], axis=0, keepdims=True))
            if start[i] is not None:
                best = jnp.maximum(best, start[i][...])
            out[...] = best


def compare(core, sets, plan, name):
    wide = sets[0][0][0].shape[1]
    rows = [sum(a.shape[0] for a in arrays) for arrays, _, _ in sets]
    vmem = pl.BlockSpec(memory_space=pltpu.VMEM)
    args = [a for arrays, _, _ in sets for a in arrays]
    args += [best for _, best, _ in sets if best is not None]
    wanted = [n for n, (_, _, want) in zip(rows, sets) if want]
    scratch = []
    for n in rows:
        scratch += [
            pltpu.VMEM((n, 128), jnp.float32),
            pltpu.VMEM((8, n), jnp.float32),
            pltpu.VMEM((n, 128), jnp.float32),
            pltpu.VMEM((8, n), jnp.float32),
        ]
    scratch += [
        pltpu.VMEM((n, wide), jnp.bfloat16)
        for n, (arrays, _, _) in zip(rows, sets)
        if len(arrays) > 1
    ]
    return pl.pallas_call(
        functools.partial(
            compare_kernel,
            plan,
            [(len(arrays), best is not None, want) for arrays, best, want in sets],
        ),
        out_shape=tuple(jax.ShapeDtypeStruct((1, n), jnp.float32) for n in wanted),
        in_specs=[pl.BlockSpec(memory_space=pltpu.SMEM)] + [vmem] * len(args),
        out_specs=(vmem,) * len(wanted),
        scratch_shapes=scratch,
        compiler_params=pltpu.CompilerParams(vmem_limit_bytes=24 * MIB),
        cost_estimate=pl.CostEstimate(
            flops=2 * len(plan) * TILE * TILE * wide,
            bytes_accessed=2 * wide * sum(rows),
            transcendentals=0,
        ),
        name=name,
    )(core, *args)


def unpack_kernel(back_ref, home_ref, slot_ref, out_ref):
    docs = home_ref.shape[1]
    on_home = lax.broadcasted_iota(jnp.int32, (CHIPS, docs), 0) == home_ref[...]
    found = lax.dot_general(
        back_ref[...],
        on_home.astype(jnp.float32),
        (((0,), (0,)), ((), ())),
        precision=lax.Precision.HIGHEST,
        preferred_element_type=jnp.float32,
    )
    in_slot = lax.broadcasted_iota(jnp.int32, (SLOTS, docs), 0) == slot_ref[...]
    out_ref[...] = jnp.sum(jnp.where(in_slot, found, 0.0), axis=0, keepdims=True)


def unpack(back, home, slot):
    vmem = pl.BlockSpec(memory_space=pltpu.VMEM)
    return pl.pallas_call(
        unpack_kernel,
        out_shape=jax.ShapeDtypeStruct(home.shape, jnp.float32),
        in_specs=[vmem] * 3,
        out_specs=vmem,
        name="unpack",
    )(back, home, slot)


def to_home(a, step):
    place = lambda z, y, c, x: ((z * NY + y) * NC + c) * NX + x
    pairs = [
        (place(z, y, c, x), place(z, (y + step * c) % NY, c, (x + step * (1 - c)) % NX))
        for z in range(NZ)
        for y in range(NY)
        for c in range(NC)
        for x in range(NX)
        if (x + y + z) % 2
    ]
    return lax.ppermute(a, ALL, pairs)


def other_core(a):
    return lax.ppermute(a, "core", [(0, 1), (1, 0)])


def exchange(a):
    return lax.all_to_all(a, TORUS, split_axis=0, concat_axis=0, tiled=True)


def per_device(embeddings, cluster, doc_rank):
    docs, features = embeddings.shape
    place = jnp.stack([lax.axis_index("core"), lax.axis_index("z") // (NZ // 2)]).astype(jnp.int32)
    core = place[:1]
    rows, home, slot = pack(place, embeddings, jnp.stack([cluster, doc_rank]))
    wide = features + 128
    near = exchange(rows.reshape(CHIPS, HALF, wide)).reshape(CHIPS * HALF, wide)
    part = near.shape[0] // 4
    quarter = [near[i * part : (i + 1) * part] for i in range(4)]
    far = [[to_home(quarter[i], 1), to_home(quarter[i + 2], -1)] for i in (0, 1)]
    near_there = other_core(near)
    plan = (
        ((0, 0), (0, 0), False),
        ((0, 1), (0, 1), False),
        ((0, 0), (0, 1), True),
        ((0, 0), (1, 1), True),
        ((0, None), (1, None), True),
    )
    best = compare(core, [([near], None, True), ([near_there], None, True)], plan, "compare_near")
    far[0], best = lax.optimization_barrier((far[0], best))
    far_there = [[other_core(a) for a in far[0]]]
    plan = (
        ((0, 0), (0, 0), False),
        *(((0, 0), (k, b), True) for k in (1, 2) for b in (0, 1)),
    )
    best_first, *best = compare(
        core,
        [(far[0], None, True), ([near], best[0], True), ([near_there], best[1], True)],
        plan,
        "compare_first",
    )
    far[1], best_first, best = lax.optimization_barrier((far[1], best_first, best))
    far_there.append([other_core(a) for a in far[1]])
    plan = (
        ((0, 0), (0, 0), False),
        *(((0, 0), (k, b), True) for k, b in ((1, 0), (2, 0), (3, 0), (3, 1), (4, 0), (4, 1))),
    )
    best_second, best_first, best_first_there, *best = compare(
        core,
        [
            (far[1], None, True),
            (far[0], best_first, True),
            (far_there[0], None, True),
            ([near], best[0], True),
            ([near_there], best[1], True),
        ],
        plan,
        "compare_second",
    )
    theirs = other_core(jnp.concatenate([best[1], best_first_there], axis=1))
    best_first, best_second = compare(
        core,
        [
            (far[0], best_first, True),
            (far[1], best_second, True),
            (far_there[0], None, False),
            (far_there[1], None, False),
        ],
        (((0, 0), (2, 0), False), ((1, 0), (3, 0), False)),
        "compare_cores",
    )
    count = near.shape[0]
    best_near = jnp.maximum(best[0], theirs[:, :count])
    best_first = jnp.maximum(best_first, theirs[:, count:])
    best_far = [b[:, i : i + part] for i in (0, part) for b in (best_first, best_second)]
    best_far = jnp.concatenate(best_far, axis=1)
    result = [b.reshape(CHIPS, HALF) for b in (best_near, best_far)]
    return unpack(exchange(jnp.concatenate(result, axis=1)), home, slot).reshape(docs)


def solution(mesh):
    torus = Mesh(mesh.devices.reshape(NZ, NY, NC, NX), ALL)
    placed = (P(ALL, None), P(ALL), P(ALL))
    return jax.shard_map(
        per_device, mesh=torus, in_specs=placed, out_specs=P(ALL), check_vma=False
    )
```

```python
import functools

import jax
import jax.numpy as jnp
from jax import lax
from jax.experimental import pallas as pl
from jax.experimental.pallas import tpu as pltpu
from jax.sharding import Mesh, PartitionSpec as P

NZ, NY, NC, NX = 8, 4, 2, 4
CHIPS = NZ * NY * NX
SLOTS = 16
HALF = 8
NO_RANK = 1 << 20
TORUS = ("z", "y", "x")
ALL = ("z", "y", "core", "x")
MIB = 2**20
TILE = 512


def dot(a, b, dims):
    return lax.dot_general(a, b, (dims, ((), ())), preferred_element_type=jnp.float32)


def digit_weights():
    which = lax.broadcasted_iota(jnp.int32, (128, 128), 0)
    weight = jnp.where(
        which == 0, 1, jnp.where(which == 1, 256, jnp.where(which == 2, 65536, -NO_RANK))
    )
    return jnp.where(which < 4, weight, 0).astype(jnp.float32).astype(jnp.bfloat16)


def pack_kernel(place_ref, emb_ref, labels_ref, rows_ref, home_ref, slot_ref):
    docs, features = emb_ref.shape
    wide = emb_ref[...].astype(jnp.float32)
    squares = jnp.sum(wide * wide, axis=1, keepdims=True) + 1e-06
    unit = (wide * lax.rsqrt(squares)).astype(jnp.bfloat16)
    clu = labels_ref[0:1, :]
    z, y, xh = clu // 8, (clu // 2) % 4, clu % 2
    x = 2 * xh + (y + z) % 2
    home = (z * NY + y) * NX + x
    on_home = lax.broadcasted_iota(jnp.int32, (CHIPS, docs), 0) == home
    member = on_home.astype(jnp.bfloat16)
    ahead = lax.broadcasted_iota(jnp.int32, (docs, docs), 0) < lax.broadcasted_iota(
        jnp.int32, (docs, docs), 1
    )
    before = dot(member, ahead.astype(jnp.bfloat16), ((1,), (0,)))
    slot = jnp.sum(jnp.where(on_home, before, 0.0), axis=0, keepdims=True).astype(jnp.int32)
    home_ref[...] = home
    slot_ref[...] = slot
    rank = labels_ref[1:2, :]
    which = lax.broadcasted_iota(jnp.int32, (128, docs), 0)
    digits = jnp.where(
        which == 0,
        rank & 255,
        jnp.where(which == 1, (rank >> 8) & 255, jnp.where(which == 2, rank >> 16, 1)),
    )
    digits = jnp.where(which < 4, digits, 0).astype(jnp.float32).astype(jnp.bfloat16)
    core, upper = place_ref[0], place_ref[1]
    side = jnp.where(upper == 0, -1, 1)
    dy, dx = side * core, side * (1 - core)
    via = (z * NY + ((y + dy) & 3)) * NX + ((x + dx) & 3)
    at = jnp.where(slot < HALF, home * HALF + slot, via * HALF + slot - HALF)
    pick = lax.broadcasted_iota(jnp.int32, (CHIPS * HALF, docs), 0) == at
    pick = jnp.where(pick, 1.0, 0.0).astype(jnp.bfloat16)
    rows_ref[:, :features] = dot(pick, unit, ((1,), (0,))).astype(jnp.bfloat16)
    rows_ref[:, features:] = dot(pick, digits, ((1,), (1,))).astype(jnp.bfloat16)


def pack(place, embeddings, labels):
    docs, features = embeddings.shape
    vmem = pl.BlockSpec(memory_space=pltpu.VMEM)
    return pl.pallas_call(
        pack_kernel,
        out_shape=(
            jax.ShapeDtypeStruct((CHIPS * HALF, features + 128), jnp.bfloat16),
            jax.ShapeDtypeStruct((1, docs), jnp.int32),
            jax.ShapeDtypeStruct((1, docs), jnp.int32),
        ),
        in_specs=[pl.BlockSpec(memory_space=pltpu.SMEM), vmem, vmem],
        out_specs=(vmem,) * 3,
        compiler_params=pltpu.CompilerParams(vmem_limit_bytes=24 * MIB),
        name="pack",
    )(place, embeddings, labels)


def compare_kernel(plan, sets, *refs):
    core_ref, refs = refs[0], list(refs[1:])
    pieces, start, outs, by_row, by_col, row_rank, col_rank, joined = ([] for _ in range(8))
    for n, _, _ in sets:
        pieces.append([refs.pop(0) for _ in range(n)])
    for _, has, _ in sets:
        start.append(refs.pop(0) if has else None)
    for _, _, wanted in sets:
        outs.append(refs.pop(0) if wanted else None)
    for _ in sets:
        by_row.append(refs.pop(0))
        by_col.append(refs.pop(0))
        row_rank.append(refs.pop(0))
        col_rank.append(refs.pop(0))
    weights = digit_weights()
    features = pieces[0][0].shape[1] - 128
    for i, (n, _, _) in enumerate(sets):
        if n > 1:
            whole = refs.pop(0)
            part = pieces[i][0].shape[0]
            for p, piece in enumerate(pieces[i]):
                whole[p * part : (p + 1) * part, :] = piece[...]
        else:
            whole = pieces[i][0]
        joined.append(whole)
        tail = whole[:, features:]
        row_rank[i][...] = dot(tail, weights, ((1,), (0,))) + float(NO_RANK)
        col_rank[i][...] = dot(weights[:, :8], tail, ((0,), (1,))) + float(NO_RANK)
        by_row[i][...] = jnp.full(by_row[i].shape, -1.0, jnp.float32)
        by_col[i][...] = jnp.full(by_col[i].shape, -1.0, jnp.float32)
    core = core_ref[0]
    for (q, qb), (k, kb), both in plan:
        q_at = pl.ds(pl.multiple_of((core if qb is None else qb) * TILE, TILE), TILE)
        k_at = pl.ds(pl.multiple_of((core if kb is None else kb) * TILE, TILE), TILE)
        scores = dot(joined[q][q_at, :features], joined[k][k_at, :features], ((1,), (1,)))
        q_rank = row_rank[q][q_at, :]
        top = by_row[q][q_at, :]
        k_rank = col_rank[k][0:1, k_at]
        side = []
        for c in range(TILE // 128):
            cols = slice(c * 128, (c + 1) * 128)
            part = scores[:, cols]
            earlier = k_rank[:, cols] < q_rank
            top = jnp.maximum(top, jnp.where(earlier, part, -1.0))
            if both:
                other = jnp.where(earlier, -1.0, part)
                side.append(jnp.max(other.reshape(TILE // 8, 8, 128), axis=0))
        by_row[q][q_at, :] = top
        if both:
            by_col[k][:, k_at] = jnp.maximum(by_col[k][:, k_at], jnp.concatenate(side, axis=1))
    for i, out in enumerate(outs):
        if out is not None:
            best = jnp.max(jnp.transpose(by_row[i][...]), axis=0, keepdims=True)
            best = jnp.maximum(best, jnp.max(by_col[i][...], axis=0, keepdims=True))
            if start[i] is not None:
                best = jnp.maximum(best, start[i][...])
            out[...] = best


def compare(core, sets, plan, name):
    wide = sets[0][0][0].shape[1]
    rows = [sum(a.shape[0] for a in arrays) for arrays, _, _ in sets]
    vmem = pl.BlockSpec(memory_space=pltpu.VMEM)
    args = [a for arrays, _, _ in sets for a in arrays]
    args += [best for _, best, _ in sets if best is not None]
    wanted = [n for n, (_, _, want) in zip(rows, sets) if want]
    scratch = []
    for n in rows:
        scratch += [
            pltpu.VMEM((n, 128), jnp.float32),
            pltpu.VMEM((8, n), jnp.float32),
            pltpu.VMEM((n, 128), jnp.float32),
            pltpu.VMEM((8, n), jnp.float32),
        ]
    scratch += [
        pltpu.VMEM((n, wide), jnp.bfloat16)
        for n, (arrays, _, _) in zip(rows, sets)
        if len(arrays) > 1
    ]
    return pl.pallas_call(
        functools.partial(
            compare_kernel,
            plan,
            [(len(arrays), best is not None, want) for arrays, best, want in sets],
        ),
        out_shape=tuple(jax.ShapeDtypeStruct((1, n), jnp.float32) for n in wanted),
        in_specs=[pl.BlockSpec(memory_space=pltpu.SMEM)] + [vmem] * len(args),
        out_specs=(vmem,) * len(wanted),
        scratch_shapes=scratch,
        compiler_params=pltpu.CompilerParams(vmem_limit_bytes=24 * MIB),
        cost_estimate=pl.CostEstimate(
            flops=2 * len(plan) * TILE * TILE * wide,
            bytes_accessed=2 * wide * sum(rows),
            transcendentals=0,
        ),
        name=name,
    )(core, *args)


def unpack_kernel(back_ref, home_ref, slot_ref, out_ref):
    docs = home_ref.shape[1]
    on_home = lax.broadcasted_iota(jnp.int32, (CHIPS, docs), 0) == home_ref[...]
    found = lax.dot_general(
        back_ref[...],
        on_home.astype(jnp.float32),
        (((0,), (0,)), ((), ())),
        precision=lax.Precision.HIGHEST,
        preferred_element_type=jnp.float32,
    )
    in_slot = lax.broadcasted_iota(jnp.int32, (SLOTS, docs), 0) == slot_ref[...]
    out_ref[...] = jnp.sum(jnp.where(in_slot, found, 0.0), axis=0, keepdims=True)


def unpack(back, home, slot):
    vmem = pl.BlockSpec(memory_space=pltpu.VMEM)
    return pl.pallas_call(
        unpack_kernel,
        out_shape=jax.ShapeDtypeStruct(home.shape, jnp.float32),
        in_specs=[vmem] * 3,
        out_specs=vmem,
        name="unpack",
    )(back, home, slot)


def to_home(a, step):
    place = lambda z, y, c, x: ((z * NY + y) * NC + c) * NX + x
    pairs = [
        (place(z, y, c, x), place(z, (y + step * c) % NY, c, (x + step * (1 - c)) % NX))
        for z in range(NZ)
        for y in range(NY)
        for c in range(NC)
        for x in range(NX)
        if (x + y + z) % 2
    ]
    return lax.ppermute(a, ALL, pairs)


def other_core(a):
    return lax.ppermute(a, "core", [(0, 1), (1, 0)])


def exchange(a):
    return lax.all_to_all(a, TORUS, split_axis=0, concat_axis=0, tiled=True)


def per_device(embeddings, cluster, doc_rank):
    docs, features = embeddings.shape
    place = jnp.stack([lax.axis_index("core"), lax.axis_index("z") // (NZ // 2)]).astype(jnp.int32)
    core = place[:1]
    rows, home, slot = pack(place, embeddings, jnp.stack([cluster, doc_rank]))
    wide = features + 128
    near = exchange(rows.reshape(CHIPS, HALF, wide)).reshape(CHIPS * HALF, wide)
    part = near.shape[0] // 4
    quarter = [near[i * part : (i + 1) * part] for i in range(4)]
    far = [[to_home(quarter[0], 1), to_home(quarter[2], -1)]]
    near_there = other_core(near)
    plan = (
        ((0, 0), (0, 0), False),
        ((0, 1), (0, 1), False),
        ((0, 0), (0, 1), True),
        ((0, 0), (1, 1), True),
        ((0, None), (1, None), True),
    )
    best = compare(core, [([near], None, True), ([near_there], None, True)], plan, "compare_near")
    later, best = lax.optimization_barrier(((quarter[1], quarter[3]), best))
    far.append([to_home(later[0], 1), to_home(later[1], -1)])
    far[0], best = lax.optimization_barrier((far[0], best))
    far_there = [[other_core(a) for a in far[0]]]
    plan = (
        ((0, 0), (0, 0), False),
        *(((0, 0), (k, b), True) for k in (1, 2) for b in (0, 1)),
    )
    best_first, *best = compare(
        core,
        [(far[0], None, True), ([near], best[0], True), ([near_there], best[1], True)],
        plan,
        "compare_first",
    )
    far[1], best_first, best = lax.optimization_barrier((far[1], best_first, best))
    far_there.append([other_core(a) for a in far[1]])
    plan = (
        ((0, 0), (0, 0), False),
        *(((0, 0), (k, b), True) for k, b in ((1, 0), (2, 0), (3, 0), (3, 1), (4, 0), (4, 1))),
    )
    best_second, best_first, best_first_there, *best = compare(
        core,
        [
            (far[1], None, True),
            (far[0], best_first, True),
            (far_there[0], None, True),
            ([near], best[0], True),
            ([near_there], best[1], True),
        ],
        plan,
        "compare_second",
    )
    theirs = other_core(jnp.concatenate([best[1], best_first_there], axis=1))
    best_first, best_second = compare(
        core,
        [
            (far[0], best_first, True),
            (far[1], best_second, True),
            (far_there[0], None, False),
            (far_there[1], None, False),
        ],
        (((0, 0), (2, 0), False), ((1, 0), (3, 0), False)),
        "compare_cores",
    )
    count = near.shape[0]
    best_near = jnp.maximum(best[0], theirs[:, :count])
    best_first = jnp.maximum(best_first, theirs[:, count:])
    best_far = [b[:, i : i + part] for i in (0, part) for b in (best_first, best_second)]
    best_far = jnp.concatenate(best_far, axis=1)
    result = [b.reshape(CHIPS, HALF) for b in (best_near, best_far)]
    return unpack(exchange(jnp.concatenate(result, axis=1)), home, slot).reshape(docs)


def solution(mesh):
    torus = Mesh(mesh.devices.reshape(NZ, NY, NC, NX), ALL)
    placed = (P(ALL, None), P(ALL), P(ALL))
    return jax.shard_map(
        per_device, mesh=torus, in_specs=placed, out_specs=P(ALL), check_vma=False
    )
```

```python
import functools

import jax
import jax.numpy as jnp
from jax import lax
from jax.experimental import pallas as pl
from jax.experimental.pallas import tpu as pltpu
from jax.sharding import Mesh, PartitionSpec as P

NZ, NY, NC, NX = 8, 4, 2, 4
CHIPS = NZ * NY * NX
SLOTS = 16
HALF = 8
NO_RANK = 1 << 20
TORUS = ("z", "y", "x")
ALL = ("z", "y", "core", "x")
MIB = 2**20
TILE = 512


def dot(a, b, dims):
    return lax.dot_general(a, b, (dims, ((), ())), preferred_element_type=jnp.float32)


def pack_kernel(place_ref, emb_ref, labels_ref, rows_ref, ranks_ref, home_ref, slot_ref):
    docs, features = emb_ref.shape
    wide = emb_ref[...].astype(jnp.float32)
    squares = jnp.sum(wide * wide, axis=1, keepdims=True) + 1e-06
    unit = (wide * lax.rsqrt(squares)).astype(jnp.bfloat16)
    clu = labels_ref[0:1, :]
    z, y, xh = clu // 8, (clu // 2) % 4, clu % 2
    x = 2 * xh + (y + z) % 2
    home = (z * NY + y) * NX + x
    on_home = lax.broadcasted_iota(jnp.int32, (CHIPS, docs), 0) == home
    member = on_home.astype(jnp.bfloat16)
    ahead = lax.broadcasted_iota(jnp.int32, (docs, docs), 0) < lax.broadcasted_iota(
        jnp.int32, (docs, docs), 1
    )
    before = dot(member, ahead.astype(jnp.bfloat16), ((1,), (0,)))
    slot = jnp.sum(jnp.where(on_home, before, 0.0), axis=0, keepdims=True).astype(jnp.int32)
    home_ref[...] = home
    slot_ref[...] = slot
    rank = labels_ref[1:2, :]
    in_slot = lax.broadcasted_iota(jnp.int32, (SLOTS, docs), 0) == slot
    digits = (rank & 255, (rank >> 8) & 255, rank >> 16, jnp.ones_like(rank))
    cols = jnp.concatenate(
        [jnp.where(in_slot, d.astype(jnp.float32), 0.0) for d in digits], axis=0
    ).astype(jnp.bfloat16)
    placed = dot(cols, member, ((1,), (1,))).astype(jnp.int32)
    low, mid, high, there = (placed[i * SLOTS : (i + 1) * SLOTS, :] for i in range(4))
    ranks_ref[...] = jnp.where(there > 0, low + 256 * mid + 65536 * high, NO_RANK)
    core, upper = place_ref[0], place_ref[1]
    side = jnp.where(upper == 0, -1, 1)
    dy, dx = side * core, side * (1 - core)
    via = (z * NY + ((y + dy) & 3)) * NX + ((x + dx) & 3)
    at = jnp.where(slot < HALF, home * HALF + slot, via * HALF + slot - HALF)
    pick = lax.broadcasted_iota(jnp.int32, (CHIPS * HALF, docs), 0) == at
    pick = jnp.where(pick, 1.0, 0.0).astype(jnp.bfloat16)
    rows_ref[...] = dot(pick, unit, ((1,), (0,))).astype(jnp.bfloat16)


def pack(place, embeddings, labels):
    docs, features = embeddings.shape
    vmem = pl.BlockSpec(memory_space=pltpu.VMEM)
    return pl.pallas_call(
        pack_kernel,
        out_shape=(
            jax.ShapeDtypeStruct((CHIPS * HALF, features), jnp.bfloat16),
            jax.ShapeDtypeStruct((SLOTS, CHIPS), jnp.int32),
            jax.ShapeDtypeStruct((1, docs), jnp.int32),
            jax.ShapeDtypeStruct((1, docs), jnp.int32),
        ),
        in_specs=[pl.BlockSpec(memory_space=pltpu.SMEM), vmem, vmem],
        out_specs=(vmem,) * 4,
        compiler_params=pltpu.CompilerParams(vmem_limit_bytes=24 * MIB),
        name="pack",
    )(place, embeddings, labels)


def spread_kernel(here_ref, there_ref, *outs):
    outs = list(outs)
    for ref in (here_ref, there_ref):
        ranks = ref[...]
        digits = [ranks & 255, (ranks >> 8) & 255, ranks >> 16]
        digits = jnp.concatenate(digits, axis=0).astype(jnp.float32).astype(jnp.bfloat16)
        for first_slot, skip, count in ((0, 0, 1024), (HALF, 0, 512), (HALF, 32, 512)):
            row = lax.broadcasted_iota(jnp.int32, (count, CHIPS), 0)
            chip = row // HALF if count == 1024 else row // HALF + row // 256 * 32 + skip
            of_chip = lax.broadcasted_iota(jnp.int32, (count, CHIPS), 1) == chip
            found = dot(jnp.where(of_chip, 1.0, 0.0).astype(jnp.bfloat16), digits, ((1,), (1,)))
            column = lax.broadcasted_iota(jnp.int32, found.shape, 1)
            own_slot = lax.broadcasted_iota(jnp.int32, found.shape, 0) % HALF + first_slot
            weight = jnp.where(column < SLOTS, 1.0, jnp.where(column < 2 * SLOTS, 256.0, 65536.0))
            found = jnp.where(column % SLOTS == own_slot, found * weight, 0.0)
            wide = jnp.broadcast_to(jnp.sum(found, axis=1, keepdims=True), (count, 128))
            outs.pop(0)[...] = jnp.transpose(wide)[0:1, :]
            if ref is here_ref:
                outs.pop(0)[...] = wide


def spread(here, there):
    vmem = pl.BlockSpec(memory_space=pltpu.VMEM)
    sizes = (1024, 512, 512)
    shapes = [shape for n in sizes for shape in ((1, n), (n, 128))] + [(1, n) for n in sizes]
    outs = pl.pallas_call(
        spread_kernel,
        out_shape=tuple(jax.ShapeDtypeStruct(shape, jnp.float32) for shape in shapes),
        in_specs=[vmem] * 2,
        out_specs=(vmem,) * len(shapes),
        compiler_params=pltpu.CompilerParams(vmem_limit_bytes=16 * MIB),
        name="spread",
    )(here, there)
    return outs[0:6:2], outs[1:6:2], outs[6:]


def swap_kernel(bit, mine_ref, kept_ref, came_ref, out_ref):
    kept, came = kept_ref[...], came_ref[...]
    mine = mine_ref[0]
    lane_bit = (lax.broadcasted_iota(jnp.int32, kept.shape, 1) // bit) & 1
    down, up = pltpu.roll(came, bit, 1), pltpu.roll(came, kept.shape[1] - bit, 1)
    out_ref[...] = jnp.where(lane_bit == mine, kept, jnp.where(mine == 0, down, up))


def swap(kept, came, bit, mine):
    vmem = pl.BlockSpec(memory_space=pltpu.VMEM)
    return pl.pallas_call(
        functools.partial(swap_kernel, bit),
        out_shape=jax.ShapeDtypeStruct(kept.shape, kept.dtype),
        in_specs=[pl.BlockSpec(memory_space=pltpu.SMEM), vmem, vmem],
        out_specs=vmem,
        name="swap",
    )(mine, kept, came)


def compare_kernel(plan, sets, *refs):
    core_ref, refs = refs[0], list(refs[1:])
    take = lambda flags: [refs.pop(0) if flag else None for flag in flags]
    pieces = [[refs.pop(0) for _ in range(n)] for n, _, _, _ in sets]
    col_rank = take([True for _ in sets])
    row_rank = take([by_row for _, by_row, _, _ in sets])
    start = take([has for _, _, has, _ in sets])
    outs = take([wanted for _, _, _, wanted in sets])
    by_row = take([True for _ in sets])
    by_col = take([True for _ in sets])
    joined = []
    for i, (n, _, _, _) in enumerate(sets):
        whole = pieces[i][0]
        if n > 1:
            whole = refs.pop(0)
            part = pieces[i][0].shape[0]
            for p, piece in enumerate(pieces[i]):
                whole[p * part : (p + 1) * part, :] = piece[...]
        joined.append(whole)
        by_row[i][...] = jnp.full(by_row[i].shape, -1.0, jnp.float32)
        by_col[i][...] = jnp.full(by_col[i].shape, -1.0, jnp.float32)
    core = core_ref[0]
    for (q, qb), (k, kb), both in plan:
        q_at = pl.ds(pl.multiple_of((core if qb is None else qb) * TILE, TILE), TILE)
        k_at = pl.ds(pl.multiple_of((core if kb is None else kb) * TILE, TILE), TILE)
        scores = dot(joined[q][q_at, :], joined[k][k_at, :], ((1,), (1,)))
        q_rank = row_rank[q][q_at, :]
        top = by_row[q][q_at, :]
        k_rank = col_rank[k][:, k_at]
        side = []
        for c in range(TILE // 128):
            cols = slice(c * 128, (c + 1) * 128)
            part = scores[:, cols]
            earlier = k_rank[:, cols] < q_rank
            top = jnp.maximum(top, jnp.where(earlier, part, -1.0))
            if both:
                other = jnp.where(earlier, -1.0, part)
                side.append(jnp.max(other.reshape(TILE // 8, 8, 128), axis=0))
        by_row[q][q_at, :] = top
        if both:
            by_col[k][:, k_at] = jnp.maximum(by_col[k][:, k_at], jnp.concatenate(side, axis=1))
    as_query = {q for (q, _), _, _ in plan}
    as_key = {k for _, (k, _), both in plan if both}
    for i, out in enumerate(outs):
        if out is None:
            continue
        best = None if start[i] is None else start[i][...]
        if i in as_query:
            found = jnp.max(jnp.transpose(by_row[i][...]), axis=0, keepdims=True)
            best = found if best is None else jnp.maximum(best, found)
        if i in as_key:
            found = jnp.max(by_col[i][...], axis=0, keepdims=True)
            best = found if best is None else jnp.maximum(best, found)
        out[...] = best


def compare(core, sets, plan, name):
    wide = sets[0][0][0].shape[1]
    rows = [sum(a.shape[0] for a in s[0]) for s in sets]
    vmem = pl.BlockSpec(memory_space=pltpu.VMEM)
    args = [a for s in sets for a in s[0]] + [s[1] for s in sets]
    args += [s[2] for s in sets if s[2] is not None] + [s[3] for s in sets if s[3] is not None]
    wanted = [n for n, s in zip(rows, sets) if s[4]]
    scratch = [pltpu.VMEM((n, 128), jnp.float32) for n in rows]
    scratch += [pltpu.VMEM((8, n), jnp.float32) for n in rows]
    scratch += [pltpu.VMEM((n, wide), jnp.bfloat16) for n, s in zip(rows, sets) if len(s[0]) > 1]
    return pl.pallas_call(
        functools.partial(
            compare_kernel,
            plan,
            [(len(s[0]), s[2] is not None, s[3] is not None, s[4]) for s in sets],
        ),
        out_shape=tuple(jax.ShapeDtypeStruct((1, n), jnp.float32) for n in wanted),
        in_specs=[pl.BlockSpec(memory_space=pltpu.SMEM)] + [vmem] * len(args),
        out_specs=(vmem,) * len(wanted),
        scratch_shapes=scratch,
        compiler_params=pltpu.CompilerParams(vmem_limit_bytes=24 * MIB),
        cost_estimate=pl.CostEstimate(
            flops=2 * len(plan) * TILE * TILE * wide,
            bytes_accessed=2 * wide * sum(rows),
            transcendentals=0,
        ),
        name=name,
    )(core, *args)


def unpack_kernel(back_ref, home_ref, slot_ref, out_ref):
    docs = home_ref.shape[1]
    on_home = lax.broadcasted_iota(jnp.int32, (CHIPS, docs), 0) == home_ref[...]
    found = lax.dot_general(
        back_ref[...],
        on_home.astype(jnp.float32),
        (((0,), (0,)), ((), ())),
        precision=lax.Precision.HIGHEST,
        preferred_element_type=jnp.float32,
    )
    in_slot = lax.broadcasted_iota(jnp.int32, (SLOTS, docs), 0) == slot_ref[...]
    out_ref[...] = jnp.sum(jnp.where(in_slot, found, 0.0), axis=0, keepdims=True)


def unpack(back, home, slot):
    vmem = pl.BlockSpec(memory_space=pltpu.VMEM)
    return pl.pallas_call(
        unpack_kernel,
        out_shape=jax.ShapeDtypeStruct(home.shape, jnp.float32),
        in_specs=[vmem] * 3,
        out_specs=vmem,
        name="unpack",
    )(back, home, slot)


def to_home(a, step):
    place = lambda z, y, c, x: ((z * NY + y) * NC + c) * NX + x
    pairs = [
        (place(z, y, c, x), place(z, (y + step * c) % NY, c, (x + step * (1 - c)) % NX))
        for z in range(NZ)
        for y in range(NY)
        for c in range(NC)
        for x in range(NX)
        if (x + y + z) % 2
    ]
    return lax.ppermute(a, ALL, pairs)


def other_core(a):
    return lax.ppermute(a, "core", [(0, 1), (1, 0)])


def exchange(a):
    return lax.all_to_all(a, TORUS, split_axis=0, concat_axis=0, tiled=True)


def exchange_small(a):
    span = CHIPS
    for axis, size in zip(TORUS, (NZ, NY, NX)):
        bit = size // 2
        while bit:
            span //= 2
            mine = (lax.axis_index(axis) // bit % 2).astype(jnp.int32).reshape(1)
            came = lax.ppermute(a, axis, [(i, i ^ bit) for i in range(size)])
            a = swap(a, came, span, mine)
            bit //= 2
    return a


def per_device(embeddings, cluster, doc_rank):
    docs, features = embeddings.shape
    place = jnp.stack([lax.axis_index("core"), lax.axis_index("z") // (NZ // 2)]).astype(jnp.int32)
    core = place[:1]
    rows, ranks, home, slot = pack(place, embeddings, jnp.stack([cluster, doc_rank]))
    near = exchange(rows.reshape(CHIPS, HALF, features)).reshape(CHIPS * HALF, features)
    ranks = exchange_small(ranks)
    cols, rank_rows, cols_there = spread(ranks, other_core(ranks))
    near, cols, rank_rows, cols_there = lax.optimization_barrier((near, cols, rank_rows, cols_there))
    near_col, *wave_col = cols
    near_col_there, *wave_col_there = cols_there
    near_row, *wave_row = rank_rows
    part = near.shape[0] // 4
    quarter = [near[i * part : (i + 1) * part] for i in range(4)]
    far = [[to_home(quarter[i], 1), to_home(quarter[i + 2], -1)] for i in (0, 1)]
    near_there = other_core(near)

    def near_sets(best, rows_too):
        return [
            ([near], near_col, near_row if rows_too else None, best[0], True),
            ([near_there], near_col_there, None, best[1], True),
        ]

    plan = (
        ((0, 0), (0, 0), False),
        ((0, 1), (0, 1), False),
        ((0, 0), (0, 1), True),
        ((0, 0), (1, 1), True),
        ((0, None), (1, None), True),
    )
    best = compare(core, near_sets((None, None), True), plan, "compare_near")
    far[0], best = lax.optimization_barrier((far[0], best))
    far_there = [[other_core(a) for a in far[0]]]
    plan = (
        ((0, 0), (0, 0), False),
        *(((0, 0), (k, b), True) for k in (1, 2) for b in (0, 1)),
    )
    best_first, *best = compare(
        core,
        [(far[0], wave_col[0], wave_row[0], None, True), *near_sets(best, False)],
        plan,
        "compare_first",
    )
    far[1], best_first, best = lax.optimization_barrier((far[1], best_first, best))
    far_there.append([other_core(a) for a in far[1]])
    plan = (
        ((0, 0), (0, 0), False),
        *(((0, 0), (k, b), True) for k, b in ((1, 0), (2, 0), (3, 0), (3, 1), (4, 0), (4, 1))),
    )
    best_second, best_first, best_first_there, *best = compare(
        core,
        [
            (far[1], wave_col[1], wave_row[1], None, True),
            (far[0], wave_col[0], None, best_first, True),
            (far_there[0], wave_col_there[0], None, None, True),
            *near_sets(best, False),
        ],
        plan,
        "compare_second",
    )
    theirs = other_core(jnp.concatenate([best[1], best_first_there], axis=1))
    best_first, best_second = compare(
        core,
        [
            (far[0], wave_col[0], wave_row[0], best_first, True),
            (far[1], wave_col[1], wave_row[1], best_second, True),
            (far_there[0], wave_col_there[0], None, None, False),
            (far_there[1], wave_col_there[1], None, None, False),
        ],
        (((0, 0), (2, 0), False), ((1, 0), (3, 0), False)),
        "compare_cores",
    )
    count = near.shape[0]
    best_near = jnp.maximum(best[0], theirs[:, :count])
    best_first = jnp.maximum(best_first, theirs[:, count:])
    best_far = [b[:, i : i + part] for i in (0, part) for b in (best_first, best_second)]
    best_far = jnp.concatenate(best_far, axis=1)
    result = [b.reshape(CHIPS, HALF) for b in (best_near, best_far)]
    return unpack(exchange(jnp.concatenate(result, axis=1)), home, slot).reshape(docs)


def solution(mesh):
    torus = Mesh(mesh.devices.reshape(NZ, NY, NC, NX), ALL)
    placed = (P(ALL, None), P(ALL), P(ALL))
    return jax.shard_map(
        per_device, mesh=torus, in_specs=placed, out_specs=P(ALL), check_vma=False
    )
```

```python
import functools

import jax
import jax.numpy as jnp
from jax import lax
from jax.experimental import pallas as pl
from jax.experimental.pallas import tpu as pltpu
from jax.sharding import Mesh, PartitionSpec as P

NZ, NY, NC, NX = 8, 4, 2, 4
CHIPS = NZ * NY * NX
CLUSTERS = CHIPS // 2
SLOTS = 16
HALF = 8
NO_RANK = 1 << 20
TORUS = ("z", "y", "xh", "xl")
PAIRS = ("z", "y", "xh")
ALL = ("z", "y", "core", "xh", "xl")
MIB = 2**20
TILE = 512


def dot(a, b, dims):
    return lax.dot_general(a, b, (dims, ((), ())), preferred_element_type=jnp.float32)


def digit_weights():
    which = lax.broadcasted_iota(jnp.int32, (128, 128), 0)
    weight = jnp.where(
        which == 0, 1, jnp.where(which == 1, 256, jnp.where(which == 2, 65536, -NO_RANK))
    )
    return jnp.where(which < 4, weight, 0).astype(jnp.float32).astype(jnp.bfloat16)


def pack_kernel(place_ref, emb_ref, labels_ref, rows_ref, slot_ref):
    docs, features = emb_ref.shape
    clu, rank = labels_ref[0:1, :], labels_ref[1:2, :]
    z, y, xh = clu // 8, (clu // 2) % 4, clu % 2
    x = 2 * xh + (y + z) % 2
    home = (z * NY + y) * NX + x
    in_cluster = lax.broadcasted_iota(jnp.int32, (CLUSTERS, docs), 0) == clu
    ahead = lax.broadcasted_iota(jnp.int32, (docs, docs), 0) < lax.broadcasted_iota(
        jnp.int32, (docs, docs), 1
    )
    before = dot(in_cluster.astype(jnp.bfloat16), ahead.astype(jnp.bfloat16), ((1,), (0,)))
    slot = jnp.sum(jnp.where(in_cluster, before, 0.0), axis=0, keepdims=True).astype(jnp.int32)
    slot_ref[...] = slot
    which = lax.broadcasted_iota(jnp.int32, (128, docs), 0)
    digits = jnp.where(
        which == 0,
        rank & 255,
        jnp.where(which == 1, (rank >> 8) & 255, jnp.where(which == 2, rank >> 16, 1)),
    )
    digits = jnp.where(which < 4, digits, 0).astype(jnp.float32).astype(jnp.bfloat16)
    core, upper = place_ref[0], place_ref[1]
    side = jnp.where(upper == 0, -1, 1)
    dy, dx = side * core, side * (1 - core)
    via = (z * NY + ((y + dy) & 3)) * NX + ((x + dx) & 3)
    at = jnp.where(slot < HALF, home * HALF + slot, via * HALF + slot - HALF)
    pick = lax.broadcasted_iota(jnp.int32, (CHIPS * HALF, docs), 0) == at
    pick = jnp.where(pick, 1.0, 0.0).astype(jnp.bfloat16)
    rows_ref[:, features:] = dot(pick, digits, ((1,), (1,))).astype(jnp.bfloat16)
    wide = emb_ref[...].astype(jnp.float32)
    squares = jnp.sum(wide * wide, axis=1, keepdims=True) + 1e-06
    unit = (wide * lax.rsqrt(squares)).astype(jnp.bfloat16)
    rows_ref[:, :features] = dot(pick, unit, ((1,), (0,))).astype(jnp.bfloat16)


def pack(place, embeddings, labels):
    docs, features = embeddings.shape
    vmem = pl.BlockSpec(memory_space=pltpu.VMEM)
    return pl.pallas_call(
        pack_kernel,
        out_shape=(
            jax.ShapeDtypeStruct((CHIPS * HALF, features + 128), jnp.bfloat16),
            jax.ShapeDtypeStruct((1, docs), jnp.int32),
        ),
        in_specs=[pl.BlockSpec(memory_space=pltpu.SMEM), vmem, vmem],
        out_specs=(vmem,) * 2,
        compiler_params=pltpu.CompilerParams(vmem_limit_bytes=24 * MIB),
        name="pack",
    )(place, embeddings, labels)


def compare_kernel(plan, sets, *refs):
    core_ref, refs = refs[0], list(refs[1:])
    pieces, start, outs, by_row, by_col, row_rank, col_rank, joined = ([] for _ in range(8))
    for n, _, _ in sets:
        pieces.append([refs.pop(0) for _ in range(n)])
    for _, has, _ in sets:
        start.append(refs.pop(0) if has else None)
    for _, _, wanted in sets:
        outs.append(refs.pop(0) if wanted else None)
    for _ in sets:
        by_row.append(refs.pop(0))
        by_col.append(refs.pop(0))
        row_rank.append(refs.pop(0))
        col_rank.append(refs.pop(0))
    weights = digit_weights()
    features = pieces[0][0].shape[1] - 128
    as_query = {q for (q, _), _, _ in plan}
    as_key = {k for _, (k, _), _ in plan}
    maximum_of_key = {k for _, (k, _), both in plan if both}
    for i, (n, _, _) in enumerate(sets):
        if n > 1:
            whole = refs.pop(0)
            part = pieces[i][0].shape[0]
            for p, piece in enumerate(pieces[i]):
                whole[p * part : (p + 1) * part, :] = piece[...]
        else:
            whole = pieces[i][0]
        joined.append(whole)
        tail = whole[:, features:]
        if i in as_query:
            row_rank[i][...] = dot(tail, weights, ((1,), (0,))) + float(NO_RANK)
            by_row[i][...] = jnp.full(by_row[i].shape, -1.0, jnp.float32)
        if i in as_key:
            col_rank[i][...] = dot(weights[:, :8], tail, ((0,), (1,))) + float(NO_RANK)
            by_col[i][...] = jnp.full(by_col[i].shape, -1.0, jnp.float32)
    core = core_ref[0]
    for (q, qb), (k, kb), both in plan:
        q_at = pl.ds(pl.multiple_of((core if qb is None else qb) * TILE, TILE), TILE)
        k_at = pl.ds(pl.multiple_of((core if kb is None else kb) * TILE, TILE), TILE)
        scores = dot(joined[q][q_at, :features], joined[k][k_at, :features], ((1,), (1,)))
        q_rank = row_rank[q][q_at, :]
        top = by_row[q][q_at, :]
        k_rank = col_rank[k][0:1, k_at]
        side = []
        for c in range(TILE // 128):
            cols = slice(c * 128, (c + 1) * 128)
            part = scores[:, cols]
            earlier = k_rank[:, cols] < q_rank
            top = jnp.maximum(top, jnp.where(earlier, part, -1.0))
            if both:
                other = jnp.where(earlier, -1.0, part)
                side.append(jnp.max(other.reshape(TILE // 8, 8, 128), axis=0))
        by_row[q][q_at, :] = top
        if both:
            by_col[k][:, k_at] = jnp.maximum(by_col[k][:, k_at], jnp.concatenate(side, axis=1))
    for i, out in enumerate(outs):
        if out is None:
            continue
        best = None if start[i] is None else start[i][...]
        if i in as_query:
            found = jnp.max(jnp.transpose(by_row[i][...]), axis=0, keepdims=True)
            best = found if best is None else jnp.maximum(best, found)
        if i in maximum_of_key:
            found = jnp.max(by_col[i][...], axis=0, keepdims=True)
            best = found if best is None else jnp.maximum(best, found)
        out[...] = best


def compare(core, sets, plan, name):
    wide = sets[0][0][0].shape[1]
    rows = [sum(a.shape[0] for a in arrays) for arrays, _, _ in sets]
    vmem = pl.BlockSpec(memory_space=pltpu.VMEM)
    args = [a for arrays, _, _ in sets for a in arrays]
    args += [best for _, best, _ in sets if best is not None]
    wanted = [n for n, (_, _, want) in zip(rows, sets) if want]
    scratch = []
    for n in rows:
        scratch += [
            pltpu.VMEM((n, 128), jnp.float32),
            pltpu.VMEM((8, n), jnp.float32),
            pltpu.VMEM((n, 128), jnp.float32),
            pltpu.VMEM((8, n), jnp.float32),
        ]
    scratch += [
        pltpu.VMEM((n, wide), jnp.bfloat16)
        for n, (arrays, _, _) in zip(rows, sets)
        if len(arrays) > 1
    ]
    return pl.pallas_call(
        functools.partial(
            compare_kernel,
            plan,
            [(len(arrays), best is not None, want) for arrays, best, want in sets],
        ),
        out_shape=tuple(jax.ShapeDtypeStruct((1, n), jnp.float32) for n in wanted),
        in_specs=[pl.BlockSpec(memory_space=pltpu.SMEM)] + [vmem] * len(args),
        out_specs=(vmem,) * len(wanted),
        scratch_shapes=scratch,
        compiler_params=pltpu.CompilerParams(vmem_limit_bytes=24 * MIB),
        cost_estimate=pl.CostEstimate(
            flops=2 * len(plan) * TILE * TILE * wide,
            bytes_accessed=2 * wide * sum(rows),
            transcendentals=0,
        ),
        name=name,
    )(core, *args)


def unpack_kernel(back_ref, clu_ref, slot_ref, out_ref):
    docs = clu_ref.shape[1]
    in_cluster = lax.broadcasted_iota(jnp.int32, (CLUSTERS, docs), 0) == clu_ref[...]
    found = lax.dot_general(
        back_ref[...],
        in_cluster.astype(jnp.float32),
        (((0,), (0,)), ((), ())),
        precision=lax.Precision.HIGHEST,
        preferred_element_type=jnp.float32,
    )
    in_slot = lax.broadcasted_iota(jnp.int32, (SLOTS, docs), 0) == slot_ref[...]
    out_ref[...] = jnp.sum(jnp.where(in_slot, found, 0.0), axis=0, keepdims=True)


def unpack(back, cluster, slot):
    vmem = pl.BlockSpec(memory_space=pltpu.VMEM)
    return pl.pallas_call(
        unpack_kernel,
        out_shape=jax.ShapeDtypeStruct(slot.shape, jnp.float32),
        in_specs=[vmem] * 3,
        out_specs=vmem,
        name="unpack",
    )(back, cluster, slot)


def to_home(a, step):
    place = lambda z, y, c, x: ((z * NY + y) * NC + c) * NX + x
    pairs = [
        (place(z, y, c, x), place(z, (y + step * c) % NY, c, (x + step * (1 - c)) % NX))
        for z in range(NZ)
        for y in range(NY)
        for c in range(NC)
        for x in range(NX)
        if (x + y + z) % 2
    ]
    return lax.ppermute(a, ALL, pairs)


def other_core(a):
    return lax.ppermute(a, "core", [(0, 1), (1, 0)])


def exchange(a, axes):
    return lax.all_to_all(a, axes, split_axis=0, concat_axis=0, tiled=True)


def per_device(embeddings, cluster, doc_rank):
    docs, features = embeddings.shape
    place = jnp.stack([lax.axis_index("core"), lax.axis_index("z") // (NZ // 2)]).astype(jnp.int32)
    core = place[:1]
    rows, slot = pack(place, embeddings, jnp.stack([cluster, doc_rank]))
    wide = features + 128
    near = exchange(rows.reshape(CHIPS, HALF, wide), TORUS).reshape(CHIPS * HALF, wide)
    part = near.shape[0] // 4
    quarter = [near[i * part : (i + 1) * part] for i in range(4)]
    far = [[to_home(quarter[i], 1), to_home(quarter[i + 2], -1)] for i in (0, 1)]
    near_there = other_core(near)
    plan = (
        ((0, 0), (0, 0), False),
        ((0, 1), (0, 1), False),
        ((0, 0), (0, 1), True),
        ((0, 0), (1, 1), True),
        ((0, None), (1, None), True),
    )
    best = compare(core, [([near], None, True), ([near_there], None, True)], plan, "compare_near")
    far[0], best = lax.optimization_barrier((far[0], best))
    far_there = [[other_core(a) for a in far[0]]]
    plan = (
        ((0, 0), (0, 0), False),
        *(((0, 0), (k, b), True) for k in (1, 2) for b in (0, 1)),
    )
    best_first, *best = compare(
        core,
        [(far[0], None, True), ([near], best[0], True), ([near_there], best[1], True)],
        plan,
        "compare_first",
    )
    far[1], best_first, best = lax.optimization_barrier((far[1], best_first, best))
    far_there.append([other_core(a) for a in far[1]])
    plan = (
        ((0, 0), (0, 0), False),
        *(((0, 0), (k, b), True) for k, b in ((1, 0), (2, 0), (3, 0), (3, 1), (4, 0), (4, 1))),
    )
    best_second, best_first, best_first_there, *best = compare(
        core,
        [
            (far[1], None, True),
            (far[0], best_first, True),
            (far_there[0], None, True),
            ([near], best[0], True),
            ([near_there], best[1], True),
        ],
        plan,
        "compare_second",
    )
    theirs = other_core(jnp.concatenate([best[1], best_first_there], axis=1))
    best_first, best_second = compare(
        core,
        [
            (far[0], best_first, True),
            (far[1], best_second, True),
            (far_there[0], None, False),
            (far_there[1], None, False),
        ],
        (((0, 0), (2, 0), False), ((1, 0), (3, 0), False)),
        "compare_cores",
    )
    count = near.shape[0]
    best_near = jnp.maximum(best[0], theirs[:, :count])
    best_first = jnp.maximum(best_first, theirs[:, count:])
    best_far = [b[:, i : i + part] for i in (0, part) for b in (best_first, best_second)]
    best_far = jnp.concatenate(best_far, axis=1)
    result = jnp.concatenate([b.reshape(CHIPS, HALF) for b in (best_near, best_far)], axis=1)
    passed = lax.ppermute(result, "xl", [(0, 1), (1, 0)])
    at_home = (lax.axis_index("xl") + lax.axis_index("y") + lax.axis_index("z")) % 2 == 0
    result = jnp.where(at_home, result, passed).reshape(CLUSTERS, 2, SLOTS)
    result = jnp.where(lax.axis_index("xl") == 0, result[:, 0], result[:, 1])
    return unpack(exchange(result, PAIRS), cluster.reshape(1, docs), slot).reshape(docs)


def solution(mesh):
    torus = Mesh(mesh.devices.reshape(NZ, NY, NC, NX // 2, 2), ALL)
    placed = (P(ALL, None), P(ALL), P(ALL))
    return jax.shard_map(
        per_device, mesh=torus, in_specs=placed, out_specs=P(ALL), check_vma=False
    )
```

```python
import functools

import jax
import jax.numpy as jnp
from jax import lax
from jax.experimental import pallas as pl
from jax.experimental.pallas import tpu as pltpu
from jax.sharding import Mesh, PartitionSpec as P

NZ, NY, NC, NX = 8, 4, 2, 4
CHIPS = NZ * NY * NX
SLOTS = 16
HALF = 8
NO_RANK = 1 << 20
TORUS = ("z", "y", "x")
ALL = ("z", "y", "core", "x")
MIB = 2**20
TILE = 512


def dot(a, b, dims):
    return lax.dot_general(a, b, (dims, ((), ())), preferred_element_type=jnp.float32)


def digit_weights():
    which = lax.broadcasted_iota(jnp.int32, (128, 128), 0)
    weight = jnp.where(
        which == 0, 1, jnp.where(which == 1, 256, jnp.where(which == 2, 65536, -NO_RANK))
    )
    return jnp.where(which < 4, weight, 0).astype(jnp.float32).astype(jnp.bfloat16)


def place_kernel(place_ref, labels_ref, at_ref, digits_ref, home_ref, slot_ref):
    docs = labels_ref.shape[1]
    clu = labels_ref[0:1, :]
    z, y, xh = clu // 8, (clu // 2) % 4, clu % 2
    x = 2 * xh + (y + z) % 2
    home = (z * NY + y) * NX + x
    in_cluster = lax.broadcasted_iota(jnp.int32, (CHIPS // 2, docs), 0) == clu
    ahead = lax.broadcasted_iota(jnp.int32, (docs, docs), 0) < lax.broadcasted_iota(
        jnp.int32, (docs, docs), 1
    )
    before = dot(in_cluster.astype(jnp.bfloat16), ahead.astype(jnp.bfloat16), ((1,), (0,)))
    slot = jnp.sum(jnp.where(in_cluster, before, 0.0), axis=0, keepdims=True).astype(jnp.int32)
    home_ref[...] = home
    slot_ref[...] = slot
    rank = labels_ref[1:2, :]
    which = lax.broadcasted_iota(jnp.int32, (128, docs), 0)
    digits = jnp.where(
        which == 0,
        rank & 255,
        jnp.where(which == 1, (rank >> 8) & 255, jnp.where(which == 2, rank >> 16, 1)),
    )
    digits_ref[...] = jnp.where(which < 4, digits, 0).astype(jnp.float32).astype(jnp.bfloat16)
    core, upper = place_ref[0], place_ref[1]
    side = jnp.where(upper == 0, -1, 1)
    dy, dx = side * core, side * (1 - core)
    via = (z * NY + ((y + dy) & 3)) * NX + ((x + dx) & 3)
    at_ref[...] = jnp.where(slot < HALF, home * HALF + slot, via * HALF + slot - HALF)


def pack_kernel(emb_ref, at_ref, digits_ref, rows_ref):
    docs, features = emb_ref.shape
    wide = emb_ref[...].astype(jnp.float32)
    squares = jnp.sum(wide * wide, axis=1, keepdims=True) + 1e-06
    unit = (wide * lax.rsqrt(squares)).astype(jnp.bfloat16)
    pick = lax.broadcasted_iota(jnp.int32, (CHIPS * HALF, docs), 0) == at_ref[...]
    pick = jnp.where(pick, 1.0, 0.0).astype(jnp.bfloat16)
    rows_ref[:, :features] = dot(pick, unit, ((1,), (0,))).astype(jnp.bfloat16)
    rows_ref[:, features:] = dot(pick, digits_ref[...], ((1,), (1,))).astype(jnp.bfloat16)


def pack(place, embeddings, labels):
    docs, features = embeddings.shape
    vmem = pl.BlockSpec(memory_space=pltpu.VMEM)
    limit = pltpu.CompilerParams(vmem_limit_bytes=24 * MIB)
    line = jax.ShapeDtypeStruct((1, docs), jnp.int32)
    at, digits, home, slot = pl.pallas_call(
        place_kernel,
        out_shape=(line, jax.ShapeDtypeStruct((128, docs), jnp.bfloat16), line, line),
        in_specs=[pl.BlockSpec(memory_space=pltpu.SMEM), vmem],
        out_specs=(vmem,) * 4,
        compiler_params=limit,
        cost_estimate=pl.CostEstimate(flops=2 * 10**9, bytes_accessed=MIB, transcendentals=0),
        name="place",
    )(place, labels)
    rows = pl.pallas_call(
        pack_kernel,
        out_shape=jax.ShapeDtypeStruct((CHIPS * HALF, features + 128), jnp.bfloat16),
        in_specs=[vmem] * 3,
        out_specs=vmem,
        compiler_params=limit,
        name="pack",
    )(embeddings, at, digits)
    return rows, home, slot


def compare_kernel(plan, sets, *refs):
    core_ref, refs = refs[0], list(refs[1:])
    pieces, start, outs, by_row, by_col, row_rank, col_rank, joined = ([] for _ in range(8))
    for n, _, _ in sets:
        pieces.append([refs.pop(0) for _ in range(n)])
    for _, has, _ in sets:
        start.append(refs.pop(0) if has else None)
    for _, _, wanted in sets:
        outs.append(refs.pop(0) if wanted else None)
    for _ in sets:
        by_row.append(refs.pop(0))
        by_col.append(refs.pop(0))
        row_rank.append(refs.pop(0))
        col_rank.append(refs.pop(0))
    weights = digit_weights()
    features = pieces[0][0].shape[1] - 128
    as_query = {q for (q, _), _, _ in plan}
    as_key = {k for _, (k, _), _ in plan}
    maximum_of_key = {k for _, (k, _), both in plan if both}
    for i, (n, _, _) in enumerate(sets):
        if n > 1:
            whole = refs.pop(0)
            part = pieces[i][0].shape[0]
            for p, piece in enumerate(pieces[i]):
                whole[p * part : (p + 1) * part, :] = piece[...]
        else:
            whole = pieces[i][0]
        joined.append(whole)
        tail = whole[:, features:]
        if i in as_query:
            row_rank[i][...] = dot(tail, weights, ((1,), (0,))) + float(NO_RANK)
            by_row[i][...] = jnp.full(by_row[i].shape, -1.0, jnp.float32)
        if i in as_key:
            col_rank[i][...] = dot(weights[:, :8], tail, ((0,), (1,))) + float(NO_RANK)
            by_col[i][...] = jnp.full(by_col[i].shape, -1.0, jnp.float32)
    core = core_ref[0]
    for (q, qb), (k, kb), both in plan:
        q_at = pl.ds(pl.multiple_of((core if qb is None else qb) * TILE, TILE), TILE)
        k_at = pl.ds(pl.multiple_of((core if kb is None else kb) * TILE, TILE), TILE)
        scores = dot(joined[q][q_at, :features], joined[k][k_at, :features], ((1,), (1,)))
        q_rank = row_rank[q][q_at, :]
        top = by_row[q][q_at, :]
        k_rank = col_rank[k][0:1, k_at]
        side = []
        for c in range(TILE // 128):
            cols = slice(c * 128, (c + 1) * 128)
            part = scores[:, cols]
            earlier = k_rank[:, cols] < q_rank
            top = jnp.maximum(top, jnp.where(earlier, part, -1.0))
            if both:
                other = jnp.where(earlier, -1.0, part)
                side.append(jnp.max(other.reshape(TILE // 8, 8, 128), axis=0))
        by_row[q][q_at, :] = top
        if both:
            by_col[k][:, k_at] = jnp.maximum(by_col[k][:, k_at], jnp.concatenate(side, axis=1))
    for i, out in enumerate(outs):
        if out is None:
            continue
        best = None if start[i] is None else start[i][...]
        if i in as_query:
            found = jnp.max(jnp.transpose(by_row[i][...]), axis=0, keepdims=True)
            best = found if best is None else jnp.maximum(best, found)
        if i in maximum_of_key:
            found = jnp.max(by_col[i][...], axis=0, keepdims=True)
            best = found if best is None else jnp.maximum(best, found)
        out[...] = best


def compare(core, sets, plan, name):
    wide = sets[0][0][0].shape[1]
    rows = [sum(a.shape[0] for a in arrays) for arrays, _, _ in sets]
    vmem = pl.BlockSpec(memory_space=pltpu.VMEM)
    args = [a for arrays, _, _ in sets for a in arrays]
    args += [best for _, best, _ in sets if best is not None]
    wanted = [n for n, (_, _, want) in zip(rows, sets) if want]
    scratch = []
    for n in rows:
        scratch += [
            pltpu.VMEM((n, 128), jnp.float32),
            pltpu.VMEM((8, n), jnp.float32),
            pltpu.VMEM((n, 128), jnp.float32),
            pltpu.VMEM((8, n), jnp.float32),
        ]
    scratch += [
        pltpu.VMEM((n, wide), jnp.bfloat16)
        for n, (arrays, _, _) in zip(rows, sets)
        if len(arrays) > 1
    ]
    return pl.pallas_call(
        functools.partial(
            compare_kernel,
            plan,
            [(len(arrays), best is not None, want) for arrays, best, want in sets],
        ),
        out_shape=tuple(jax.ShapeDtypeStruct((1, n), jnp.float32) for n in wanted),
        in_specs=[pl.BlockSpec(memory_space=pltpu.SMEM)] + [vmem] * len(args),
        out_specs=(vmem,) * len(wanted),
        scratch_shapes=scratch,
        compiler_params=pltpu.CompilerParams(vmem_limit_bytes=24 * MIB),
        cost_estimate=pl.CostEstimate(
            flops=2 * len(plan) * TILE * TILE * wide,
            bytes_accessed=2 * wide * sum(rows),
            transcendentals=0,
        ),
        name=name,
    )(core, *args)


def unpack_kernel(back_ref, home_ref, slot_ref, out_ref):
    docs = home_ref.shape[1]
    on_home = lax.broadcasted_iota(jnp.int32, (CHIPS, docs), 0) == home_ref[...]
    found = lax.dot_general(
        back_ref[...],
        on_home.astype(jnp.float32),
        (((0,), (0,)), ((), ())),
        precision=lax.Precision.HIGHEST,
        preferred_element_type=jnp.float32,
    )
    in_slot = lax.broadcasted_iota(jnp.int32, (SLOTS, docs), 0) == slot_ref[...]
    out_ref[...] = jnp.sum(jnp.where(in_slot, found, 0.0), axis=0, keepdims=True)


def unpack(back, home, slot):
    vmem = pl.BlockSpec(memory_space=pltpu.VMEM)
    return pl.pallas_call(
        unpack_kernel,
        out_shape=jax.ShapeDtypeStruct(home.shape, jnp.float32),
        in_specs=[vmem] * 3,
        out_specs=vmem,
        name="unpack",
    )(back, home, slot)


def to_home(a, step):
    place = lambda z, y, c, x: ((z * NY + y) * NC + c) * NX + x
    pairs = [
        (place(z, y, c, x), place(z, (y + step * c) % NY, c, (x + step * (1 - c)) % NX))
        for z in range(NZ)
        for y in range(NY)
        for c in range(NC)
        for x in range(NX)
        if (x + y + z) % 2
    ]
    return lax.ppermute(a, ALL, pairs)


def other_core(a):
    return lax.ppermute(a, "core", [(0, 1), (1, 0)])


def exchange(a):
    return lax.all_to_all(a, TORUS, split_axis=0, concat_axis=0, tiled=True)


def per_device(embeddings, cluster, doc_rank):
    docs, features = embeddings.shape
    place = jnp.stack([lax.axis_index("core"), lax.axis_index("z") // (NZ // 2)]).astype(jnp.int32)
    core = place[:1]
    rows, home, slot = pack(place, embeddings, jnp.stack([cluster, doc_rank]))
    wide = features + 128
    near = exchange(rows.reshape(CHIPS, HALF, wide)).reshape(CHIPS * HALF, wide)
    part = near.shape[0] // 4
    quarter = [near[i * part : (i + 1) * part] for i in range(4)]
    far = [[to_home(quarter[i], 1), to_home(quarter[i + 2], -1)] for i in (0, 1)]
    near_there = other_core(near)
    plan = (
        ((0, 0), (0, 0), False),
        ((0, 1), (0, 1), False),
        ((0, 0), (0, 1), True),
        ((0, 0), (1, 1), True),
        ((0, None), (1, None), True),
    )
    best = compare(core, [([near], None, True), ([near_there], None, True)], plan, "compare_near")
    far[0], best = lax.optimization_barrier((far[0], best))
    far_there = [[other_core(a) for a in far[0]]]
    plan = (
        ((0, 0), (0, 0), False),
        *(((0, 0), (k, b), True) for k in (1, 2) for b in (0, 1)),
    )
    best_first, *best = compare(
        core,
        [(far[0], None, True), ([near], best[0], True), ([near_there], best[1], True)],
        plan,
        "compare_first",
    )
    far[1], best_first, best = lax.optimization_barrier((far[1], best_first, best))
    far_there.append([other_core(a) for a in far[1]])
    plan = (
        ((0, 0), (0, 0), False),
        *(((0, 0), (k, b), True) for k, b in ((1, 0), (2, 0), (3, 0), (3, 1), (4, 0), (4, 1))),
    )
    best_second, best_first, best_first_there, *best = compare(
        core,
        [
            (far[1], None, True),
            (far[0], best_first, True),
            (far_there[0], None, True),
            ([near], best[0], True),
            ([near_there], best[1], True),
        ],
        plan,
        "compare_second",
    )
    theirs = other_core(jnp.concatenate([best[1], best_first_there], axis=1))
    best_first, best_second = compare(
        core,
        [
            (far[0], best_first, True),
            (far[1], best_second, True),
            (far_there[0], None, False),
            (far_there[1], None, False),
        ],
        (((0, 0), (2, 0), False), ((1, 0), (3, 0), False)),
        "compare_cores",
    )
    count = near.shape[0]
    best_near = jnp.maximum(best[0], theirs[:, :count])
    best_first = jnp.maximum(best_first, theirs[:, count:])
    best_far = [b[:, i : i + part] for i in (0, part) for b in (best_first, best_second)]
    best_far = jnp.concatenate(best_far, axis=1)
    result = [b.reshape(CHIPS, HALF) for b in (best_near, best_far)]
    return unpack(exchange(jnp.concatenate(result, axis=1)), home, slot).reshape(docs)


def solution(mesh):
    torus = Mesh(mesh.devices.reshape(NZ, NY, NC, NX), ALL)
    placed = (P(ALL, None), P(ALL), P(ALL))
    return jax.shard_map(
        per_device, mesh=torus, in_specs=placed, out_specs=P(ALL), check_vma=False
    )
```

```python
import functools

import jax
import jax.numpy as jnp
from jax import lax
from jax.experimental import pallas as pl
from jax.experimental.pallas import tpu as pltpu
from jax.sharding import Mesh, PartitionSpec as P

NZ, NY, NC, NX = 8, 4, 2, 4
CHIPS = NZ * NY * NX
SLOTS = 16
HALF = 8
NO_RANK = 1 << 20
TORUS = ("y", "z", "x")
ALL = ("z", "y", "core", "x")
MIB = 2**20
TILE = 512


def dot(a, b, dims):
    return lax.dot_general(a, b, (dims, ((), ())), preferred_element_type=jnp.float32)


def digit_weights():
    which = lax.broadcasted_iota(jnp.int32, (128, 128), 0)
    weight = jnp.where(
        which == 0, 1, jnp.where(which == 1, 256, jnp.where(which == 2, 65536, -NO_RANK))
    )
    return jnp.where(which < 4, weight, 0).astype(jnp.float32).astype(jnp.bfloat16)


def place_kernel(place_ref, labels_ref, at_ref, digits_ref, home_ref, slot_ref):
    docs = labels_ref.shape[1]
    clu = labels_ref[0:1, :]
    z, y, xh = clu // 8, (clu // 2) % 4, clu % 2
    x = 2 * xh + (y + z) % 2
    home = (y * NZ + z) * NX + x
    in_cluster = lax.broadcasted_iota(jnp.int32, (CHIPS // 2, docs), 0) == clu
    ahead = lax.broadcasted_iota(jnp.int32, (docs, docs), 0) < lax.broadcasted_iota(
        jnp.int32, (docs, docs), 1
    )
    before = dot(in_cluster.astype(jnp.bfloat16), ahead.astype(jnp.bfloat16), ((1,), (0,)))
    slot = jnp.sum(jnp.where(in_cluster, before, 0.0), axis=0, keepdims=True).astype(jnp.int32)
    home_ref[...] = home
    slot_ref[...] = slot
    rank = labels_ref[1:2, :]
    which = lax.broadcasted_iota(jnp.int32, (128, docs), 0)
    digits = jnp.where(
        which == 0,
        rank & 255,
        jnp.where(which == 1, (rank >> 8) & 255, jnp.where(which == 2, rank >> 16, 1)),
    )
    digits_ref[...] = jnp.where(which < 4, digits, 0).astype(jnp.float32).astype(jnp.bfloat16)
    core, upper = place_ref[0], place_ref[1]
    side = jnp.where(upper == 0, -1, 1)
    dy, dx = side * core, side * (1 - core)
    via = (((y + dy) & 3) * NZ + z) * NX + ((x + dx) & 3)
    at_ref[...] = jnp.where(slot < HALF, home * HALF + slot, via * HALF + slot - HALF)


def pack_kernel(emb_ref, at_ref, digits_ref, rows_ref):
    docs, features = emb_ref.shape
    wide = emb_ref[...].astype(jnp.float32)
    squares = jnp.sum(wide * wide, axis=1, keepdims=True) + 1e-06
    unit = (wide * lax.rsqrt(squares)).astype(jnp.bfloat16)
    pick = lax.broadcasted_iota(jnp.int32, (CHIPS * HALF, docs), 0) == at_ref[...]
    pick = jnp.where(pick, 1.0, 0.0).astype(jnp.bfloat16)
    rows_ref[:, :features] = dot(pick, unit, ((1,), (0,))).astype(jnp.bfloat16)
    rows_ref[:, features:] = dot(pick, digits_ref[...], ((1,), (1,))).astype(jnp.bfloat16)


def pack(place, embeddings, labels):
    docs, features = embeddings.shape
    vmem = pl.BlockSpec(memory_space=pltpu.VMEM)
    limit = pltpu.CompilerParams(vmem_limit_bytes=24 * MIB)
    line = jax.ShapeDtypeStruct((1, docs), jnp.int32)
    at, digits, home, slot = pl.pallas_call(
        place_kernel,
        out_shape=(line, jax.ShapeDtypeStruct((128, docs), jnp.bfloat16), line, line),
        in_specs=[pl.BlockSpec(memory_space=pltpu.SMEM), vmem],
        out_specs=(vmem,) * 4,
        compiler_params=limit,
        cost_estimate=pl.CostEstimate(flops=2 * 10**9, bytes_accessed=MIB, transcendentals=0),
        name="place",
    )(place, labels)
    rows = pl.pallas_call(
        pack_kernel,
        out_shape=jax.ShapeDtypeStruct((CHIPS * HALF, features + 128), jnp.bfloat16),
        in_specs=[vmem] * 3,
        out_specs=vmem,
        compiler_params=limit,
        name="pack",
    )(embeddings, at, digits)
    return rows, home, slot


def compare_kernel(plan, sets, *refs):
    core_ref, refs = refs[0], list(refs[1:])
    pieces, start, outs, by_row, by_col, row_rank, col_rank, joined = ([] for _ in range(8))
    for n, _, _ in sets:
        pieces.append([refs.pop(0) for _ in range(n)])
    for _, has, _ in sets:
        start.append(refs.pop(0) if has else None)
    for _, _, wanted in sets:
        outs.append(refs.pop(0) if wanted else None)
    for _ in sets:
        by_row.append(refs.pop(0))
        by_col.append(refs.pop(0))
        row_rank.append(refs.pop(0))
        col_rank.append(refs.pop(0))
    weights = digit_weights()
    features = pieces[0][0].shape[1] - 128
    as_query = {q for (q, _), _, _ in plan}
    as_key = {k for _, (k, _), _ in plan}
    maximum_of_key = {k for _, (k, _), both in plan if both}
    for i, (n, _, _) in enumerate(sets):
        if n > 1:
            whole = refs.pop(0)
            part = pieces[i][0].shape[0]
            for p, piece in enumerate(pieces[i]):
                whole[p * part : (p + 1) * part, :] = piece[...]
        else:
            whole = pieces[i][0]
        joined.append(whole)
        tail = whole[:, features:]
        if i in as_query:
            row_rank[i][...] = dot(tail, weights, ((1,), (0,))) + float(NO_RANK)
            by_row[i][...] = jnp.full(by_row[i].shape, -1.0, jnp.float32)
        if i in as_key:
            col_rank[i][...] = dot(weights[:, :8], tail, ((0,), (1,))) + float(NO_RANK)
            by_col[i][...] = jnp.full(by_col[i].shape, -1.0, jnp.float32)
    core = core_ref[0]
    for (q, qb), (k, kb), both in plan:
        q_at = pl.ds(pl.multiple_of((core if qb is None else qb) * TILE, TILE), TILE)
        k_at = pl.ds(pl.multiple_of((core if kb is None else kb) * TILE, TILE), TILE)
        scores = dot(joined[q][q_at, :features], joined[k][k_at, :features], ((1,), (1,)))
        q_rank = row_rank[q][q_at, :]
        top = by_row[q][q_at, :]
        k_rank = col_rank[k][0:1, k_at]
        side = []
        for c in range(TILE // 128):
            cols = slice(c * 128, (c + 1) * 128)
            part = scores[:, cols]
            earlier = k_rank[:, cols] < q_rank
            top = jnp.maximum(top, jnp.where(earlier, part, -1.0))
            if both:
                other = jnp.where(earlier, -1.0, part)
                side.append(jnp.max(other.reshape(TILE // 8, 8, 128), axis=0))
        by_row[q][q_at, :] = top
        if both:
            by_col[k][:, k_at] = jnp.maximum(by_col[k][:, k_at], jnp.concatenate(side, axis=1))
    for i, out in enumerate(outs):
        if out is None:
            continue
        best = None if start[i] is None else start[i][...]
        if i in as_query:
            found = jnp.max(jnp.transpose(by_row[i][...]), axis=0, keepdims=True)
            best = found if best is None else jnp.maximum(best, found)
        if i in maximum_of_key:
            found = jnp.max(by_col[i][...], axis=0, keepdims=True)
            best = found if best is None else jnp.maximum(best, found)
        out[...] = best


def compare(core, sets, plan, name):
    wide = sets[0][0][0].shape[1]
    rows = [sum(a.shape[0] for a in arrays) for arrays, _, _ in sets]
    vmem = pl.BlockSpec(memory_space=pltpu.VMEM)
    args = [a for arrays, _, _ in sets for a in arrays]
    args += [best for _, best, _ in sets if best is not None]
    wanted = [n for n, (_, _, want) in zip(rows, sets) if want]
    scratch = []
    for n in rows:
        scratch += [
            pltpu.VMEM((n, 128), jnp.float32),
            pltpu.VMEM((8, n), jnp.float32),
            pltpu.VMEM((n, 128), jnp.float32),
            pltpu.VMEM((8, n), jnp.float32),
        ]
    scratch += [
        pltpu.VMEM((n, wide), jnp.bfloat16)
        for n, (arrays, _, _) in zip(rows, sets)
        if len(arrays) > 1
    ]
    return pl.pallas_call(
        functools.partial(
            compare_kernel,
            plan,
            [(len(arrays), best is not None, want) for arrays, best, want in sets],
        ),
        out_shape=tuple(jax.ShapeDtypeStruct((1, n), jnp.float32) for n in wanted),
        in_specs=[pl.BlockSpec(memory_space=pltpu.SMEM)] + [vmem] * len(args),
        out_specs=(vmem,) * len(wanted),
        scratch_shapes=scratch,
        compiler_params=pltpu.CompilerParams(vmem_limit_bytes=24 * MIB),
        cost_estimate=pl.CostEstimate(
            flops=2 * len(plan) * TILE * TILE * wide,
            bytes_accessed=2 * wide * sum(rows),
            transcendentals=0,
        ),
        name=name,
    )(core, *args)


def unpack_kernel(back_ref, home_ref, slot_ref, out_ref):
    docs = home_ref.shape[1]
    on_home = lax.broadcasted_iota(jnp.int32, (CHIPS, docs), 0) == home_ref[...]
    found = lax.dot_general(
        back_ref[...],
        on_home.astype(jnp.float32),
        (((0,), (0,)), ((), ())),
        precision=lax.Precision.HIGHEST,
        preferred_element_type=jnp.float32,
    )
    in_slot = lax.broadcasted_iota(jnp.int32, (SLOTS, docs), 0) == slot_ref[...]
    out_ref[...] = jnp.sum(jnp.where(in_slot, found, 0.0), axis=0, keepdims=True)


def unpack(back, home, slot):
    vmem = pl.BlockSpec(memory_space=pltpu.VMEM)
    return pl.pallas_call(
        unpack_kernel,
        out_shape=jax.ShapeDtypeStruct(home.shape, jnp.float32),
        in_specs=[vmem] * 3,
        out_specs=vmem,
        name="unpack",
    )(back, home, slot)


def to_home(a, step):
    place = lambda z, y, c, x: ((z * NY + y) * NC + c) * NX + x
    pairs = [
        (place(z, y, c, x), place(z, (y + step * c) % NY, c, (x + step * (1 - c)) % NX))
        for z in range(NZ)
        for y in range(NY)
        for c in range(NC)
        for x in range(NX)
        if (x + y + z) % 2
    ]
    return lax.ppermute(a, ALL, pairs)


def other_core(a):
    return lax.ppermute(a, "core", [(0, 1), (1, 0)])


def exchange(a):
    return lax.all_to_all(a, TORUS, split_axis=0, concat_axis=0, tiled=True)


def per_device(embeddings, cluster, doc_rank):
    docs, features = embeddings.shape
    place = jnp.stack([lax.axis_index("core"), lax.axis_index("y") // (NY // 2)]).astype(jnp.int32)
    core = place[:1]
    rows, home, slot = pack(place, embeddings, jnp.stack([cluster, doc_rank]))
    wide = features + 128
    near = exchange(rows.reshape(CHIPS, HALF, wide)).reshape(CHIPS * HALF, wide)
    part = near.shape[0] // 4
    quarter = [near[i * part : (i + 1) * part] for i in range(4)]
    far = [[to_home(quarter[i], 1), to_home(quarter[i + 2], -1)] for i in (0, 1)]
    near_there = other_core(near)
    plan = (
        ((0, 0), (0, 0), False),
        ((0, 1), (0, 1), False),
        ((0, 0), (0, 1), True),
        ((0, 0), (1, 1), True),
        ((0, None), (1, None), True),
    )
    best = compare(core, [([near], None, True), ([near_there], None, True)], plan, "compare_near")
    far[0], best = lax.optimization_barrier((far[0], best))
    far_there = [[other_core(a) for a in far[0]]]
    plan = (
        ((0, 0), (0, 0), False),
        *(((0, 0), (k, b), True) for k in (1, 2) for b in (0, 1)),
    )
    best_first, *best = compare(
        core,
        [(far[0], None, True), ([near], best[0], True), ([near_there], best[1], True)],
        plan,
        "compare_first",
    )
    far[1], best_first, best = lax.optimization_barrier((far[1], best_first, best))
    far_there.append([other_core(a) for a in far[1]])
    plan = (
        ((0, 0), (0, 0), False),
        *(((0, 0), (k, b), True) for k, b in ((1, 0), (2, 0), (3, 0), (3, 1), (4, 0), (4, 1))),
    )
    best_second, best_first, best_first_there, *best = compare(
        core,
        [
            (far[1], None, True),
            (far[0], best_first, True),
            (far_there[0], None, True),
            ([near], best[0], True),
            ([near_there], best[1], True),
        ],
        plan,
        "compare_second",
    )
    theirs = other_core(jnp.concatenate([best[1], best_first_there], axis=1))
    best_first, best_second = compare(
        core,
        [
            (far[0], best_first, True),
            (far[1], best_second, True),
            (far_there[0], None, False),
            (far_there[1], None, False),
        ],
        (((0, 0), (2, 0), False), ((1, 0), (3, 0), False)),
        "compare_cores",
    )
    count = near.shape[0]
    best_near = jnp.maximum(best[0], theirs[:, :count])
    best_first = jnp.maximum(best_first, theirs[:, count:])
    best_far = [b[:, i : i + part] for i in (0, part) for b in (best_first, best_second)]
    best_far = jnp.concatenate(best_far, axis=1)
    result = [b.reshape(CHIPS, HALF) for b in (best_near, best_far)]
    return unpack(exchange(jnp.concatenate(result, axis=1)), home, slot).reshape(docs)


def solution(mesh):
    torus = Mesh(mesh.devices.reshape(NZ, NY, NC, NX), ALL)
    placed = (P(ALL, None), P(ALL), P(ALL))
    return jax.shard_map(
        per_device, mesh=torus, in_specs=placed, out_specs=P(ALL), check_vma=False
    )
```

```python
import functools

import jax
import jax.numpy as jnp
from jax import lax
from jax.experimental import pallas as pl
from jax.experimental.pallas import tpu as pltpu
from jax.sharding import Mesh, PartitionSpec as P

NZ, NY, NC, NX = 8, 4, 2, 4
CHIPS = NZ * NY * NX
SLOTS = 16
HALF = 8
NO_RANK = 1 << 20
TORUS = ("y", "z", "x")
ALL = ("z", "y", "core", "x")
MIB = 2**20
TILE = 512


def dot(a, b, dims):
    return lax.dot_general(a, b, (dims, ((), ())), preferred_element_type=jnp.float32)


def digit_weights():
    which = lax.broadcasted_iota(jnp.int32, (128, 128), 0)
    weight = jnp.where(
        which == 0, 1, jnp.where(which == 1, 256, jnp.where(which == 2, 65536, -NO_RANK))
    )
    return jnp.where(which < 4, weight, 0).astype(jnp.float32).astype(jnp.bfloat16)


def place_kernel(place_ref, labels_ref, at_ref, digits_ref, home_ref, slot_ref):
    docs = labels_ref.shape[1]
    clu = labels_ref[0:1, :]
    z, y, xh = clu // 8, (clu // 2) % 4, clu % 2
    x = 2 * xh + (y + z) % 2
    home = (y * NZ + z) * NX + x
    in_cluster = lax.broadcasted_iota(jnp.int32, (CHIPS // 2, docs), 0) == clu
    ahead = lax.broadcasted_iota(jnp.int32, (docs, docs), 0) < lax.broadcasted_iota(
        jnp.int32, (docs, docs), 1
    )
    before = dot(in_cluster.astype(jnp.bfloat16), ahead.astype(jnp.bfloat16), ((1,), (0,)))
    slot = jnp.sum(jnp.where(in_cluster, before, 0.0), axis=0, keepdims=True).astype(jnp.int32)
    home_ref[...] = home
    slot_ref[...] = slot
    rank = labels_ref[1:2, :]
    which = lax.broadcasted_iota(jnp.int32, (128, docs), 0)
    digits = jnp.where(
        which == 0,
        rank & 255,
        jnp.where(which == 1, (rank >> 8) & 255, jnp.where(which == 2, rank >> 16, 1)),
    )
    digits_ref[...] = jnp.where(which < 4, digits, 0).astype(jnp.float32).astype(jnp.bfloat16)
    core, upper = place_ref[0], place_ref[1]
    side = jnp.where(upper == 0, -1, 1)
    dy, dx = side * core, side * (1 - core)
    via = (((y + dy) & 3) * NZ + z) * NX + ((x + dx) & 3)
    at_ref[...] = jnp.where(slot < HALF, home * HALF + slot, via * HALF + slot - HALF)


def pack_kernel(emb_ref, at_ref, digits_ref, rows_ref):
    docs, features = emb_ref.shape
    wide = emb_ref[...].astype(jnp.float32)
    squares = jnp.sum(wide * wide, axis=1, keepdims=True) + 1e-06
    unit = (wide * lax.rsqrt(squares)).astype(jnp.bfloat16)
    pick = lax.broadcasted_iota(jnp.int32, (CHIPS * HALF, docs), 0) == at_ref[...]
    pick = jnp.where(pick, 1.0, 0.0).astype(jnp.bfloat16)
    rows_ref[:, :features] = dot(pick, unit, ((1,), (0,))).astype(jnp.bfloat16)
    rows_ref[:, features:] = dot(pick, digits_ref[...], ((1,), (1,))).astype(jnp.bfloat16)


def pack(place, embeddings, labels):
    docs, features = embeddings.shape
    vmem = pl.BlockSpec(memory_space=pltpu.VMEM)
    limit = pltpu.CompilerParams(vmem_limit_bytes=24 * MIB)
    line = jax.ShapeDtypeStruct((1, docs), jnp.int32)
    at, digits, home, slot = pl.pallas_call(
        place_kernel,
        out_shape=(line, jax.ShapeDtypeStruct((128, docs), jnp.bfloat16), line, line),
        in_specs=[pl.BlockSpec(memory_space=pltpu.SMEM), vmem],
        out_specs=(vmem,) * 4,
        compiler_params=limit,
        cost_estimate=pl.CostEstimate(flops=2 * 10**9, bytes_accessed=MIB, transcendentals=0),
        name="place",
    )(place, labels)
    rows = pl.pallas_call(
        pack_kernel,
        out_shape=jax.ShapeDtypeStruct((CHIPS * HALF, features + 128), jnp.bfloat16),
        in_specs=[vmem] * 3,
        out_specs=vmem,
        compiler_params=limit,
        name="pack",
    )(embeddings, at, digits)
    return rows, home, slot


def compare_kernel(plan, sets, *refs):
    core_ref, refs = refs[0], list(refs[1:])
    pieces, start, outs, by_row, by_col, row_rank, col_rank, joined = ([] for _ in range(8))
    for n, _, _ in sets:
        pieces.append([refs.pop(0) for _ in range(n)])
    for _, has, _ in sets:
        start.append(refs.pop(0) if has else None)
    for _, _, wanted in sets:
        outs.append(refs.pop(0) if wanted else None)
    for _ in sets:
        by_row.append(refs.pop(0))
        by_col.append(refs.pop(0))
        row_rank.append(refs.pop(0))
        col_rank.append(refs.pop(0))
    weights = digit_weights()
    features = pieces[0][0].shape[1] - 128
    as_query = {q for (q, _), _, _ in plan}
    as_key = {k for _, (k, _), _ in plan}
    maximum_of_key = {k for _, (k, _), both in plan if both}
    for i, (n, _, _) in enumerate(sets):
        if n > 1:
            whole = refs.pop(0)
            part = pieces[i][0].shape[0]
            for p, piece in enumerate(pieces[i]):
                whole[p * part : (p + 1) * part, :] = piece[...]
        else:
            whole = pieces[i][0]
        joined.append(whole)
        tail = whole[:, features:]
        if i in as_query:
            row_rank[i][...] = dot(tail, weights, ((1,), (0,))) + float(NO_RANK)
            by_row[i][...] = jnp.full(by_row[i].shape, -1.0, jnp.float32)
        if i in as_key:
            col_rank[i][...] = dot(weights[:, :8], tail, ((0,), (1,))) + float(NO_RANK)
            by_col[i][...] = jnp.full(by_col[i].shape, -1.0, jnp.float32)
    core = core_ref[0]
    for (q, qb), (k, kb), both in plan:
        q_at = pl.ds(pl.multiple_of((core if qb is None else qb) * TILE, TILE), TILE)
        k_at = pl.ds(pl.multiple_of((core if kb is None else kb) * TILE, TILE), TILE)
        scores = dot(joined[q][q_at, :features], joined[k][k_at, :features], ((1,), (1,)))
        q_rank = row_rank[q][q_at, :]
        top = by_row[q][q_at, :]
        k_rank = col_rank[k][0:1, k_at]
        side = []
        for c in range(TILE // 128):
            cols = slice(c * 128, (c + 1) * 128)
            part = scores[:, cols]
            earlier = k_rank[:, cols] < q_rank
            top = jnp.maximum(top, jnp.where(earlier, part, -1.0))
            if both:
                other = jnp.where(earlier, -1.0, part)
                side.append(jnp.max(other.reshape(TILE // 8, 8, 128), axis=0))
        by_row[q][q_at, :] = top
        if both:
            by_col[k][:, k_at] = jnp.maximum(by_col[k][:, k_at], jnp.concatenate(side, axis=1))
    for i, out in enumerate(outs):
        if out is None:
            continue
        best = None if start[i] is None else start[i][...]
        if i in as_query:
            found = jnp.max(jnp.transpose(by_row[i][...]), axis=0, keepdims=True)
            best = found if best is None else jnp.maximum(best, found)
        if i in maximum_of_key:
            found = jnp.max(by_col[i][...], axis=0, keepdims=True)
            best = found if best is None else jnp.maximum(best, found)
        out[...] = best


def compare(core, sets, plan, name):
    wide = sets[0][0][0].shape[1]
    rows = [sum(a.shape[0] for a in arrays) for arrays, _, _ in sets]
    vmem = pl.BlockSpec(memory_space=pltpu.VMEM)
    args = [a for arrays, _, _ in sets for a in arrays]
    args += [best for _, best, _ in sets if best is not None]
    wanted = [n for n, (_, _, want) in zip(rows, sets) if want]
    scratch = []
    for n in rows:
        scratch += [
            pltpu.VMEM((n, 128), jnp.float32),
            pltpu.VMEM((8, n), jnp.float32),
            pltpu.VMEM((n, 128), jnp.float32),
            pltpu.VMEM((8, n), jnp.float32),
        ]
    scratch += [
        pltpu.VMEM((n, wide), jnp.bfloat16)
        for n, (arrays, _, _) in zip(rows, sets)
        if len(arrays) > 1
    ]
    return pl.pallas_call(
        functools.partial(
            compare_kernel,
            plan,
            [(len(arrays), best is not None, want) for arrays, best, want in sets],
        ),
        out_shape=tuple(jax.ShapeDtypeStruct((1, n), jnp.float32) for n in wanted),
        in_specs=[pl.BlockSpec(memory_space=pltpu.SMEM)] + [vmem] * len(args),
        out_specs=(vmem,) * len(wanted),
        scratch_shapes=scratch,
        compiler_params=pltpu.CompilerParams(vmem_limit_bytes=24 * MIB),
        cost_estimate=pl.CostEstimate(
            flops=2 * len(plan) * TILE * TILE * wide,
            bytes_accessed=2 * wide * sum(rows),
            transcendentals=0,
        ),
        name=name,
    )(core, *args)


def unpack_kernel(back_ref, home_ref, slot_ref, out_ref):
    docs = home_ref.shape[1]
    on_home = lax.broadcasted_iota(jnp.int32, (CHIPS, docs), 0) == home_ref[...]
    found = lax.dot_general(
        back_ref[...],
        on_home.astype(jnp.float32),
        (((0,), (0,)), ((), ())),
        precision=lax.Precision.HIGHEST,
        preferred_element_type=jnp.float32,
    )
    in_slot = lax.broadcasted_iota(jnp.int32, (SLOTS, docs), 0) == slot_ref[...]
    out_ref[...] = jnp.sum(jnp.where(in_slot, found, 0.0), axis=0, keepdims=True)


def unpack(back, home, slot):
    vmem = pl.BlockSpec(memory_space=pltpu.VMEM)
    return pl.pallas_call(
        unpack_kernel,
        out_shape=jax.ShapeDtypeStruct(home.shape, jnp.float32),
        in_specs=[vmem] * 3,
        out_specs=vmem,
        name="unpack",
    )(back, home, slot)


def to_home(a, step):
    place = lambda z, y, c, x: ((z * NY + y) * NC + c) * NX + x
    pairs = [
        (place(z, y, c, x), place(z, (y + step * c) % NY, c, (x + step * (1 - c)) % NX))
        for z in range(NZ)
        for y in range(NY)
        for c in range(NC)
        for x in range(NX)
        if (x + y + z) % 2
    ]
    return lax.ppermute(a, ALL, pairs)


def other_core(a):
    return lax.ppermute(a, "core", [(0, 1), (1, 0)])


def exchange(a):
    return lax.all_to_all(a, TORUS, split_axis=0, concat_axis=0, tiled=True)


def per_device(embeddings, cluster, doc_rank):
    docs, features = embeddings.shape
    place = jnp.stack([lax.axis_index("core"), lax.axis_index("y") // (NY // 2)]).astype(jnp.int32)
    core = place[:1]
    rows, home, slot = pack(place, embeddings, jnp.stack([cluster, doc_rank]))
    wide = features + 128
    near = exchange(rows.reshape(CHIPS, HALF, wide)).reshape(CHIPS * HALF, wide)
    part = near.shape[0] // 4
    quarter = [near[i * part : (i + 1) * part] for i in range(4)]
    far = [[to_home(quarter[i], 1), to_home(quarter[i + 2], -1)] for i in (0, 1)]
    near_there = other_core(near)
    plan = (
        ((0, 0), (0, 0), False),
        ((0, 1), (0, 1), False),
        ((0, 0), (0, 1), True),
        ((0, 0), (1, 1), True),
        ((0, None), (1, None), True),
    )
    best = compare(core, [([near], None, True), ([near_there], None, True)], plan, "compare_near")
    far[0], best = lax.optimization_barrier((far[0], best))
    far_there = [[other_core(a) for a in far[0]]]
    plan = (
        ((0, 0), (0, 0), False),
        *(((0, 0), (k, b), True) for k in (1, 2) for b in (0, 1)),
    )
    best_first, *best = compare(
        core,
        [(far[0], None, True), ([near], best[0], True), ([near_there], best[1], True)],
        plan,
        "compare_first",
    )
    far[1], best_first, best = lax.optimization_barrier((far[1], best_first, best))
    far_there.append([other_core(a) for a in far[1]])
    plan = (
        ((0, 0), (0, 0), False),
        *(((0, 0), (k, b), True) for k, b in ((1, 0), (2, 0), (3, 0), (3, 1), (4, 0), (4, 1))),
        ((1, 0), (2, 0), False),
    )
    best_second, best_first, best_first_there, *best = compare(
        core,
        [
            (far[1], None, True),
            (far[0], best_first, True),
            (far_there[0], None, True),
            ([near], best[0], True),
            ([near_there], best[1], True),
        ],
        plan,
        "compare_second",
    )
    theirs = other_core(jnp.concatenate([best[1], best_first_there], axis=1))
    [best_second] = compare(
        core,
        [(far[1], best_second, True), (far_there[1], None, False)],
        (((0, 0), (1, 0), False),),
        "compare_cores",
    )
    count = near.shape[0]
    best_near = jnp.maximum(best[0], theirs[:, :count])
    best_first = jnp.maximum(best_first, theirs[:, count:])
    best_far = [b[:, i : i + part] for i in (0, part) for b in (best_first, best_second)]
    best_far = jnp.concatenate(best_far, axis=1)
    result = [b.reshape(CHIPS, HALF) for b in (best_near, best_far)]
    return unpack(exchange(jnp.concatenate(result, axis=1)), home, slot).reshape(docs)


def solution(mesh):
    torus = Mesh(mesh.devices.reshape(NZ, NY, NC, NX), ALL)
    placed = (P(ALL, None), P(ALL), P(ALL))
    return jax.shard_map(
        per_device, mesh=torus, in_specs=placed, out_specs=P(ALL), check_vma=False
    )
```
